256 devices in a mesh: row: 8 (over z_lo, y), col: 4 (over z_hi), depth: 8 (over x, core).
Axes of the slice: x: 4, y: 4, z: 8 (z_hi: 4, z_lo: 2; z = z_hi * 2 + z_lo), core: 2. Of those that a mesh axis runs over, the one named last changes fastest.
Arguments:
- tokens: bfloat16 [2048, 12288], P(('row', 'col'), 'depth'), may hold values from -6 to 6
- weight: bfloat16 [12288, 24576], P('depth', ('row', 'col')), may hold values from -5 to 5
- moment: bfloat16 [12288, 24576], P('depth', ('row', 'col')), may hold values from -0.59765625 to 0.59765625
- upstream: bfloat16 [8, 256, 24576], P(None, 'col', ('row', 'depth')), may hold values from -24 to 24
Outputs:
- activated: bfloat16 [8, 256, 24576], P(None, 'col', ('row', 'depth'))
- new_weight: bfloat16 [12288, 24576], P('depth', ('row', 'col'))
- new_moment: bfloat16 [12288, 24576], P('depth', ('row', 'col'))
The draws below stay inside these ranges and needn't reach their ends.
All inputs are finite; a program needn't handle non-finite values.
Results may differ from the reference program's by a relative error of at most 0.015.
Values may be sent and summed in bfloat16 or wider, within the bound.
A program may use at most 64 MiB of HBM per device.

```python
import jax
import jax.numpy as jnp
from jax import lax

D = 12288
FF = 24576
TOK_DEV = 64
TOKENS = 2048
N_ROW = 8
N_COL = 4
N_DEPTH = 8


def block_scale(rng, shape, pieces, smallest, high):
    def one(axis_at, parts):
        steps = jax.random.uniform(jax.random.fold_in(jax.random.fold_in(rng, 6), axis_at), (parts,), jnp.float32, smallest / len(pieces), high / len(pieces))
        return jnp.repeat(jnp.exp(steps), shape[axis_at] // parts).reshape((-1,) + (1,) * (len(shape) - axis_at - 1))

    loudness = one(*pieces[0])
    for cut in pieces[1:]:
        loudness = loudness * one(*cut)
    return loudness


def bell_draw(key, extent, scale, reach, cuts=(), kind=jnp.bfloat16):
    entries = scale * jax.random.normal(key, extent, jnp.float32)
    if cuts:
        entries = entries * block_scale(key, extent, cuts, -0.22, 0.18)
    return jnp.clip(entries, -reach, reach).astype(kind)


def setup_inputs(seed: int = 0) -> dict:
    keys = jax.random.split(jax.random.key(seed), 5)
    return {
        "tokens": bell_draw(keys[0], (TOKENS, D), 1.0, 6.0, ((0, 32), (1, 8))),
        "weight": bell_draw(keys[1], (D, FF), 1.0, 5.0, ((0, 8), (1, 32))),
        "moment": bell_draw(keys[2], (D, FF), 0.1, 0.59765625, ((0, 8), (1, 32))),
        "upstream": bell_draw(keys[3], (N_ROW, N_COL * TOK_DEV, FF), 4.0, 24.0, ((1, 4), (2, 64))),
    }


gelu_coef = 0.7978845608028654
cubic_coef = 0.044715
lion_rate = 0.5
decay_rate = 0.1
beta_one = 0.9
beta_two = 0.99
smooth_tau = 0.1

def gelu_pair(preact):
    tangent = jnp.tanh(gelu_coef * (preact + cubic_coef * preact * preact * preact))
    gelu_value = 0.5 * preact * (1.0 + tangent)
    gelu_slope = 0.5 * (1.0 + tangent) + 0.5 * preact * (1.0 - tangent * tangent) * gelu_coef * (1.0 + 3.0 * cubic_coef * preact * preact)
    return (gelu_value, gelu_slope)

def reference(tokens, weight, moment, upstream):
    block_width = D // N_DEPTH
    tokens_f = tokens.astype(jnp.float32)
    weight_f = weight.astype(jnp.float32)
    summed = jnp.zeros((TOKENS, FF), jnp.float32)
    for block in range(N_DEPTH):
        part = jnp.dot(tokens_f[:, block * block_width:(block + 1) * block_width], weight_f[block * block_width:(block + 1) * block_width, :], precision=lax.Precision.HIGHEST)
        summed = summed + lax.optimization_barrier(part.astype(jnp.bfloat16)).astype(jnp.float32)
    fan_scale = D ** (-0.5)
    gelu_value, gelu_slope = gelu_pair(summed * fan_scale)
    activated = gelu_value.astype(jnp.bfloat16).reshape(N_ROW, N_COL * TOK_DEV, FF)
    upstream_flat = upstream.reshape(TOKENS, FF).astype(jnp.float32)
    act_grad = (upstream_flat * gelu_slope).astype(jnp.bfloat16)
    grad_full = lax.dot_general(tokens_f, act_grad.astype(jnp.float32), (((0,), (0,)), ((), ())), precision=lax.Precision.HIGHEST) * fan_scale
    moment_f = moment.astype(jnp.float32)
    blended = beta_one * moment_f + (1.0 - beta_one) * grad_full
    update = blended / jnp.sqrt(blended * blended + smooth_tau * smooth_tau)
    new_weight = (weight_f - lion_rate * (update + decay_rate * weight_f)).astype(jnp.bfloat16)
    new_moment = (beta_two * moment_f + (1.0 - beta_two) * grad_full).astype(jnp.bfloat16)
    return (activated, new_weight, new_moment)
```

```python
import jax
import jax.numpy as jnp
from jax import lax
from jax.sharding import PartitionSpec as P

D = 12288


gelu_coef = 0.7978845608028654
cubic_coef = 0.044715
lion_rate = 0.5
decay_rate = 0.1
beta_one = 0.9
beta_two = 0.99
smooth_tau = 0.1


def gelu_pair(preact):
    tangent = jnp.tanh(gelu_coef * (preact + cubic_coef * preact * preact * preact))
    gelu_value = 0.5 * preact * (1.0 + tangent)
    gelu_slope = 0.5 * (1.0 + tangent) + 0.5 * preact * (1.0 - tangent * tangent) * gelu_coef * (
        1.0 + 3.0 * cubic_coef * preact * preact
    )
    return (gelu_value, gelu_slope)


def shards(tokens, weight, moment, upstream):
    rows = lax.axis_size("row")
    cols = lax.axis_size("col")
    depth = lax.axis_size("depth")
    tok = tokens.shape[0]
    half = upstream.shape[2]
    cores = depth // cols
    fan_scale = D ** (-0.5)
    there = [
        (c * depth + x * cores + b, x * depth + c * cores + b)
        for c in range(cols)
        for x in range(cols)
        for b in range(cores)
    ]
    back = [(to, fro) for fro, to in there]
    up = lax.ppermute(upstream, ("col", "depth"), there)
    gathered = lax.all_gather(tokens, ("row", "col"), axis=0, tiled=True)
    partial_value = jnp.dot(gathered, weight, preferred_element_type=jnp.float32).astype(jnp.bfloat16)
    blocks = partial_value.reshape(rows, cols, tok, cores, half).transpose(1, 3, 0, 2, 4)
    summed = lax.psum_scatter(
        blocks.reshape(depth * rows * tok, half), "depth", scatter_dimension=0, tiled=True
    ).astype(jnp.float32)
    gelu_value, gelu_slope = gelu_pair(summed * fan_scale)
    activated = gelu_value.astype(jnp.bfloat16).reshape(upstream.shape)
    activated = lax.ppermute(activated, ("col", "depth"), back)
    local_grad = (up.reshape(rows * tok, half).astype(jnp.float32) * gelu_slope).astype(jnp.bfloat16)
    act_grad = lax.all_gather(local_grad, "depth", axis=0, tiled=True)
    act_grad = act_grad.reshape(cols, cores, rows, tok, half).transpose(2, 0, 3, 1, 4)
    act_grad = act_grad.reshape(rows * cols * tok, cores * half)
    grad_full = fan_scale * lax.dot_general(
        gathered, act_grad, (((0,), (0,)), ((), ())), preferred_element_type=jnp.float32
    )
    moment_f = moment.astype(jnp.float32)
    weight_f = weight.astype(jnp.float32)
    blended = beta_one * moment_f + (1.0 - beta_one) * grad_full
    update = blended / jnp.sqrt(blended * blended + smooth_tau * smooth_tau)
    new_weight = (weight_f - lion_rate * (update + decay_rate * weight_f)).astype(jnp.bfloat16)
    new_moment = (beta_two * moment_f + (1.0 - beta_two) * grad_full).astype(jnp.bfloat16)
    return (activated, new_weight, new_moment)


def solution(mesh):
    placed = (
        P(("row", "col"), "depth"),
        P("depth", ("row", "col")),
        P("depth", ("row", "col")),
        P(None, "col", ("row", "depth")),
    )
    return jax.shard_map(
        shards,
        mesh=mesh,
        in_specs=placed,
        out_specs=(
            P(None, "col", ("row", "depth")),
            P("depth", ("row", "col")),
            P("depth", ("row", "col")),
        ),
        check_vma=False,
    )
```

```python
import jax
import jax.numpy as jnp
from jax import lax
from jax.experimental import pallas as pl
from jax.experimental.pallas import tpu as pltpu
from jax.sharding import PartitionSpec as P

D = 12288
TOK = 64
KA = 1024
KB = 512
FEAT = 1536
HID = 768
HALF = 384
PIECE = 256
NSEM = 176

gelu_coef = 0.7978845608028654
cubic_coef = 0.044715
lion_rate = 0.5
decay_rate = 0.1
beta_one = 0.9
beta_two = 0.99
smooth_tau = 0.1
fan_scale = D ** (-0.5)

MESH = pl.DeviceIdType.MESH


def gelu_pair(preact):
    tangent = jnp.tanh(gelu_coef * (preact + cubic_coef * preact * preact * preact))
    gelu_value = 0.5 * preact * (1.0 + tangent)
    gelu_slope = 0.5 * (1.0 + tangent) + 0.5 * preact * (1.0 - tangent * tangent) * gelu_coef * (
        1.0 + 3.0 * cubic_coef * preact * preact
    )
    return (gelu_value, gelu_slope)


def kernel(
    tok_hbm, w_hbm, m_hbm, up_hbm,
    act_hbm, nw_hbm, nm_hbm,
    xa, xb, wv, mv, acc, own, give, got, part, share, grads, up1, up2, val2, val1,
    send_sem, recv_sem, load_sem, store_sem, act_sem,
):
    row, col, depth = lax.axis_index("row"), lax.axis_index("col"), lax.axis_index("depth")
    y, zlo = lax.rem(row, 4), row // 4
    z = col * 2 + zlo
    x, core = depth // 2, lax.rem(depth, 2)

    def at(y_, z_, x_, core_):
        return (lax.rem(z_, 2) * 4 + y_, z_ // 2, x_ * 2 + core_)

    def y_to(k):
        return at(lax.rem(y + k, 4), z, x, core)

    def z_to(k):
        return at(y, lax.rem(z + k, 8), x, core)

    def x_to(k):
        return at(y, z, lax.rem(x + k, 4), core)

    def col_to(k):
        return (row, lax.rem(col + k, 4), depth)

    partner = at(y, z, x, 1 - core)
    numbers = {}
    sent = {}

    def copy(name, src, dst, device):
        n = numbers.setdefault(name, len(numbers))
        return pltpu.make_async_remote_copy(
            src_ref=src, dst_ref=dst, send_sem=send_sem.at[n], recv_sem=recv_sem.at[n],
            device_id=device, device_id_type=MESH,
        )

    def send(name, src, dst, device):
        c = copy(name, src, dst, device)
        c.start()
        sent[name] = c

    def arrive(name, dst):
        copy(name, dst, dst, partner).wait_recv()

    mine = pl.ds(pl.multiple_of(core * HALF, 128), HALF)
    theirs = pl.ds(pl.multiple_of((1 - core) * HALF, 128), HALF)
    halves = ((mine, pl.ds(0, HALF)), (theirs, pl.ds(HALF, HALF)))
    loads = [
        pltpu.make_async_copy(tok_hbm.at[:, pl.ds(0, KA)], xa.at[0, pl.ds(0, TOK)], load_sem.at[0]),
        pltpu.make_async_copy(tok_hbm.at[:, pl.ds(KA, KB)], xb.at[0, pl.ds(0, TOK)], load_sem.at[1]),
    ]
    for i, (there, here) in enumerate(halves):
        loads.append(pltpu.make_async_copy(w_hbm.at[:, there], wv.at[:, here], load_sem.at[2 + i]))
    for i, (there, here) in enumerate(halves):
        loads.append(pltpu.make_async_copy(m_hbm.at[:, there], mv.at[:, here], load_sem.at[4 + i]))

    def home_row(x_of, x_home):
        return lax.rem(y + x_of + col + 4 - x_home, 4)

    loads.append(pltpu.make_async_copy(up_hbm.at[:, home_row(x, x)], up1.at[x], load_sem.at[6]))
    for c in loads:
        c.start()

    barrier = pltpu.get_barrier_semaphore()
    others = (
        [y_to(1), y_to(3), z_to(1), z_to(7), partner]
        + [x_to(k) for k in (1, 2, 3)]
        + [col_to(k) for k in (1, 2, 3)]
    )
    for other in others:
        pl.semaphore_signal(barrier, inc=1, device_id=other, device_id_type=MESH)
    pl.semaphore_wait(barrier, len(others))

    LOW, HIGH = pl.ds(0, 32), pl.ds(32, 32)

    def rows(dy, lo=0, n=TOK):
        return pl.ds(dy * TOK + lo, n)

    def a_along_z(k):
        down, up = (k - 1) % 8, (1 - k) % 8
        if k < 4:
            send(("az-", k), xa.at[down, rows(0)], xa.at[k, rows(0)], z_to(7))
            send(("az+", k), xa.at[up, rows(0)], xa.at[8 - k, rows(0)], z_to(1))
        else:
            send(("az-", 4), xa.at[3, LOW], xa.at[4, LOW], z_to(7))
            send(("az+", 4), xa.at[5, HIGH], xa.at[4, HIGH], z_to(1))

    def a_from_z(k):
        if k < 4:
            arrive(("az-", k), xa.at[k, rows(0)])
            arrive(("az+", k), xa.at[8 - k, rows(0)])
        else:
            arrive(("az-", 4), xa.at[4, LOW])
            arrive(("az+", 4), xa.at[4, HIGH])

    def a_along_y(dz):
        send(("ay-", dz), xa.at[dz, rows(0)], xa.at[dz, rows(1)], y_to(3))
        send(("ay+", dz), xa.at[dz, rows(0)], xa.at[dz, rows(3)], y_to(1))

    def a_from_y(dz):
        arrive(("ay-", dz), xa.at[dz, rows(1)])
        arrive(("ay+", dz), xa.at[dz, rows(3)])

    def a_far_y(dz):
        send(("af-", dz), xa.at[dz, rows(1, 0, 32)], xa.at[dz, rows(2, 0, 32)], y_to(3))
        send(("af+", dz), xa.at[dz, rows(3, 32, 32)], xa.at[dz, rows(2, 32, 32)], y_to(1))

    def a_from_far(dz):
        arrive(("af-", dz), xa.at[dz, rows(2, 0, 32)])
        arrive(("af+", dz), xa.at[dz, rows(2, 32, 32)])

    def b_along_y():
        send("by-", xb.at[0, rows(0)], xb.at[0, rows(1)], y_to(3))
        send("by+", xb.at[0, rows(0)], xb.at[0, rows(3)], y_to(1))

    def b_far_y():
        arrive("by-", xb.at[0, rows(1)])
        arrive("by+", xb.at[0, rows(3)])
        send("bf-", xb.at[0, rows(1, 0, 32)], xb.at[0, rows(2, 0, 32)], y_to(3))
        send("bf+", xb.at[0, rows(3, 32, 32)], xb.at[0, rows(2, 32, 32)], y_to(1))

    def b_from_far():
        arrive("bf-", xb.at[0, rows(2, 0, 32)])
        arrive("bf+", xb.at[0, rows(2, 32, 32)])

    def b_along_z(k):
        down, up = (k - 1) % 8, (1 - k) % 8
        if k < 4:
            send(("bz-", k), xb.at[down], xb.at[k], z_to(7))
            send(("bz+", k), xb.at[up], xb.at[8 - k], z_to(1))
        else:
            send(("bz-", 4), xb.at[3, pl.ds(0, 128)], xb.at[4, pl.ds(0, 128)], z_to(7))
            send(("bz+", 4), xb.at[5, pl.ds(128, 128)], xb.at[4, pl.ds(128, 128)], z_to(1))

    def b_from_z(k):
        if k < 4:
            arrive(("bz-", k), xb.at[k])
            arrive(("bz+", k), xb.at[8 - k])
        else:
            arrive(("bz-", 4), xb.at[4, pl.ds(0, 128)])
            arrive(("bz+", 4), xb.at[4, pl.ds(128, 128)])

    def up_along_x():
        for k in (1, 2, 3):
            there = lax.rem(x + k, 4)
            send(("ux", k), up_hbm.at[:, home_row(there, x)], up1.at[x], x_to(k))

    def up_along_z():
        loads[6].wait()
        for k in (1, 2, 3):
            arrive(("ux", k), up1.at[lax.rem(x + 4 - k, 4)])
        for k in (1, 2, 3):
            send(("uz", k), up1.at[lax.rem(col + k, 4)], up2.at[4 - k], col_to(k))
        pltpu.make_async_copy(up1.at[col], up2.at[0], load_sem.at[7]).start()

    def up_from_z():
        pltpu.make_async_copy(up1.at[col], up2.at[0], load_sem.at[7]).wait()
        for k in (1, 2, 3):
            arrive(("uz", k), up2.at[4 - k])

    def act_along_z(delta):
        if delta == 0:
            c = pltpu.make_async_copy(val2.at[0], val1.at[col], act_sem.at[0])
            c.start()
            sent["act0"] = None
        else:
            send(("vz", delta), val2.at[delta], val1.at[col], col_to(delta))

    def act_along_x():
        pltpu.make_async_copy(val2.at[0], val1.at[col], act_sem.at[0]).wait()
        for delta in (1, 3, 2):
            arrive(("vz", delta), val1.at[lax.rem(col + 4 - delta, 4)])
        for k in (1, 2, 3):
            there = lax.rem(x + k, 4)
            send(("vx", k), val1.at[there], act_hbm.at[:, home_row(x, there)], x_to(k))
        pltpu.make_async_copy(val1.at[x], act_hbm.at[:, home_row(x, x)], act_sem.at[1]).start()

    def act_done():
        pltpu.make_async_copy(val1.at[x], act_hbm.at[:, home_row(x, x)], act_sem.at[1]).wait()
        for k in (1, 2, 3):
            arrive(("vx", k), act_hbm.at[:, home_row(lax.rem(x + 4 - k, 4), x)])

    def delta_of(dz):
        return lax.rem((zlo + dz) // 2, 4)

    def chunk_rows(dz, x_of):
        dy = lax.rem(x_of + delta_of(dz), 4)
        return pl.ds(pl.multiple_of(dy * TOK, TOK), TOK)

    def forward(dz):
        for n in range(3):
            columns = pl.ds(n * 256, 256)
            value = jnp.dot(xa[dz], wv[pl.ds(0, KA), columns], preferred_element_type=jnp.float32)
            value = value + jnp.dot(xb[dz], wv[pl.ds(KA, KB), columns], preferred_element_type=jnp.float32)
            if n == 0:
                own[dz, :, pl.ds(0, 256)] = value
            elif n == 1:
                own[dz, :, pl.ds(256, 128)] = value[:, :128]
                give[dz, :, pl.ds(0, 128)] = value[:, 128:].astype(jnp.bfloat16)
            else:
                give[dz, :, pl.ds(128, 256)] = value.astype(jnp.bfloat16)
        send(("pair", dz), give.at[dz], got.at[dz], partner)

    def scatter(dz):
        arrive(("pair", dz), got.at[dz])
        total = own[dz] + got[dz].astype(jnp.float32)
        own[dz] = total
        part[dz] = total.astype(jnp.bfloat16)
        for k in (1, 2, 3):
            chunk = chunk_rows(dz, lax.rem(x + k, 4))
            send(("sum", dz, k), part.at[dz, chunk], share.at[dz, k - 1], x_to(k))

    def middle(dz):
        for k in (1, 2, 3):
            arrive(("sum", dz, k), share.at[dz, k - 1])
        chunk = chunk_rows(dz, x)
        summed = own[dz, chunk, :]
        for k in range(3):
            summed = summed + share[dz, k].astype(jnp.float32)
        gelu_value, gelu_slope = gelu_pair(summed * fan_scale)
        delta, odd = delta_of(dz), lax.rem(zlo + dz, 2)
        val2[delta, odd] = gelu_value.astype(jnp.bfloat16)
        grads[dz, 0, chunk, :] = (up2[delta, odd].astype(jnp.float32) * gelu_slope).astype(jnp.bfloat16)
        for k in (1, 2, 3):
            send(("grad", dz, k), grads.at[dz, 0, chunk], grads.at[dz, 0, chunk], x_to(k))

    def pass_on(dz):
        for k in (1, 2, 3):
            arrive(("grad", dz, k), grads.at[dz, 0, chunk_rows(dz, lax.rem(x + 4 - k, 4))])
        send(("both", dz), grads.at[dz, 0], grads.at[dz, 1], partner)

    def gradient_tile(dz, tile):
        both = jnp.concatenate([grads[dz, 0], grads[dz, 1]], axis=1)
        if isinstance(tile, tuple):
            source, columns = tile
        return lax.dot_general(
            source[dz, :, columns], both, (((0,), (0,)), ((), ())), preferred_element_type=jnp.float32
        )

    TILE = 256

    def backward(dz, first=False):
        arrive(("both", dz), grads.at[dz, 1])
        for source, base, count in ((xa, 0, KA // TILE), (xb, KA, KB // TILE)):
            @pl.loop(0, count)
            def _(t):
                columns = pl.ds(pl.multiple_of(t * TILE, TILE), TILE)
                out = pl.ds(pl.multiple_of(base + t * TILE, TILE), TILE)
                value = gradient_tile(dz, (source, columns))
                acc[out, :] = value if first else acc[out, :] + value

    def stores(tile):
        out = pl.ds(pl.multiple_of(tile * TILE, TILE), TILE)
        result = []
        for i, (there, here) in enumerate(halves):
            result.append(pltpu.make_async_copy(wv.at[out, here], nw_hbm.at[out, there], store_sem.at[tile, i]))
            result.append(pltpu.make_async_copy(mv.at[out, here], nm_hbm.at[out, there], store_sem.at[tile, 2 + i]))
        return result

    def finish(dz):
        arrive(("both", dz), grads.at[dz, 1])
        for c in loads[4:6]:
            c.wait()
        for source, base, count in ((xa, 0, KA // TILE), (xb, KA, KB // TILE)):
            @pl.loop(0, count)
            def _(t):
                columns = pl.ds(pl.multiple_of(t * TILE, TILE), TILE)
                out = pl.ds(pl.multiple_of(base + t * TILE, TILE), TILE)
                grad_full = fan_scale * (acc[out, :] + gradient_tile(dz, (source, columns)))
                moment_f = mv[out, :].astype(jnp.float32)
                weight_f = wv[out, :].astype(jnp.float32)
                blended = beta_one * moment_f + (1.0 - beta_one) * grad_full
                update = blended * lax.rsqrt(blended * blended + smooth_tau * smooth_tau)
                wv[out, :] = (weight_f - lion_rate * (update + decay_rate * weight_f)).astype(jnp.bfloat16)
                mv[out, :] = (beta_two * moment_f + (1.0 - beta_two) * grad_full).astype(jnp.bfloat16)
                for c in stores(base // TILE + t):
                    c.start()

    loads[0].wait()
    a_along_z(1)
    loads[1].wait()
    b_along_y()
    a_along_y(0)
    up_along_x()
    b_far_y()
    a_from_z(1)
    a_along_z(2)
    a_along_y(1)
    a_along_y(7)
    b_from_far()
    b_along_z(1)
    up_along_z()
    a_from_y(0)
    a_far_y(0)
    a_from_z(2)
    a_along_z(3)
    a_along_y(2)
    a_along_y(6)
    a_from_far(0)
    for c in loads[2:4]:
        c.wait()
    forward(0)
    for dz in (1, 7):
        a_from_y(dz)
        a_far_y(dz)
    b_from_z(1)
    b_along_z(2)
    scatter(0)
    a_from_z(3)
    a_along_z(4)
    a_along_y(3)
    a_along_y(5)
    a_from_far(1)
    forward(1)
    a_from_far(7)
    forward(7)
    up_from_z()
    middle(0)
    scatter(1)
    scatter(7)
    for dz in (2, 6):
        a_from_y(dz)
        a_far_y(dz)
    b_from_z(2)
    b_along_z(3)
    pass_on(0)
    a_from_z(4)
    a_along_y(4)
    middle(1)
    middle(7)
    act_along_z(0)
    a_from_far(2)
    forward(2)
    a_from_far(6)
    forward(6)
    pass_on(1)
    pass_on(7)
    backward(0, True)
    scatter(2)
    scatter(6)
    for dz in (3, 5):
        a_from_y(dz)
        a_far_y(dz)
    b_from_z(3)
    b_along_z(4)
    middle(2)
    middle(6)
    backward(1)
    backward(7)
    a_from_far(3)
    forward(3)
    a_from_far(5)
    forward(5)
    pass_on(2)
    pass_on(6)
    a_from_y(4)
    a_far_y(4)
    scatter(3)
    scatter(5)
    backward(2)
    backward(6)
    middle(3)
    act_along_z(1)
    middle(5)
    act_along_z(3)
    b_from_z(4)
    a_from_far(4)
    forward(4)
    pass_on(3)
    pass_on(5)
    scatter(4)
    backward(3)
    middle(4)
    act_along_z(2)
    backward(5)
    pass_on(4)
    act_along_x()
    finish(4)
    act_done()
    for tile in range(FEAT // TILE):
        for c in stores(tile):
            c.wait()
    for c in sent.values():
        if c is not None:
            c.wait_send()
    assert len(numbers) <= NSEM, len(numbers)


def shards(tokens, weight, moment, upstream):
    bf16, f32 = jnp.bfloat16, jnp.float32
    any_space = pl.BlockSpec(memory_space=pl.ANY)
    act, new_weight, new_moment = pl.pallas_call(
        kernel,
        out_shape=(
            jax.ShapeDtypeStruct((2, 4, TOK, HALF), bf16),
            jax.ShapeDtypeStruct((FEAT, HID), bf16),
            jax.ShapeDtypeStruct((FEAT, HID), bf16),
        ),
        in_specs=[any_space] * 4,
        out_specs=(any_space,) * 3,
        scratch_shapes=[
            pltpu.VMEM((8, PIECE, KA), bf16),
            pltpu.VMEM((8, PIECE, KB), bf16),
            pltpu.VMEM((FEAT, HID), bf16),
            pltpu.VMEM((FEAT, HID), bf16),
            pltpu.VMEM((FEAT, HID), f32),
            pltpu.VMEM((8, PIECE, HALF), f32),
            pltpu.VMEM((8, PIECE, HALF), bf16),
            pltpu.VMEM((8, PIECE, HALF), bf16),
            pltpu.VMEM((8, PIECE, HALF), bf16),
            pltpu.VMEM((8, 3, TOK, HALF), bf16),
            pltpu.VMEM((8, 2, PIECE, HALF), bf16),
            pltpu.VMEM((4, 2, TOK, HALF), bf16),
            pltpu.VMEM((4, 2, TOK, HALF), bf16),
            pltpu.VMEM((4, 2, TOK, HALF), bf16),
            pltpu.VMEM((4, 2, TOK, HALF), bf16),
            pltpu.SemaphoreType.DMA((NSEM,)),
            pltpu.SemaphoreType.DMA((NSEM,)),
            pltpu.SemaphoreType.DMA((8,)),
            pltpu.SemaphoreType.DMA((FEAT // 256, 4)),
            pltpu.SemaphoreType.DMA((2,)),
        ],
        compiler_params=pltpu.CompilerParams(
            collective_id=0, has_side_effects=True, vmem_limit_bytes=56 * 1024 * 1024
        ),
        cost_estimate=pl.CostEstimate(
            flops=4 * 2048 * FEAT * HID, bytes_accessed=12 * 1024 * 1024, transcendentals=2 * FEAT * HID
        ),
    )(tokens, weight, moment, upstream.reshape(2, 4, TOK, HALF))
    return (act.reshape(upstream.shape), new_weight, new_moment)


def solution(mesh):
    placed = (
        P(("row", "col"), "depth"),
        P("depth", ("row", "col")),
        P("depth", ("row", "col")),
        P(None, "col", ("row", "depth")),
    )
    return jax.shard_map(
        shards,
        mesh=mesh,
        in_specs=placed,
        out_specs=(
            P(None, "col", ("row", "depth")),
            P("depth", ("row", "col")),
            P("depth", ("row", "col")),
        ),
        check_vma=False,
    )
```

```python
import functools

import jax
import jax.numpy as jnp
from jax import lax
from jax.experimental import pallas as pl
from jax.experimental.pallas import tpu as pltpu
from jax.sharding import PartitionSpec as P

D = 12288
TOK = 64
KA = 1024
KB = 512
FEAT = 1536
HID = 768
HALF = 384
PIECE = 256
NSEM = 176
UPDATE = 256

gelu_coef = 0.7978845608028654
cubic_coef = 0.044715
lion_rate = 0.5
decay_rate = 0.1
beta_one = 0.9
beta_two = 0.99
smooth_tau = 0.1
fan_scale = D ** (-0.5)

MESH = pl.DeviceIdType.MESH

ORDER = (
    "start", "bfar", "bz10", "az2", "ay1", "af0", "ay7", "u0", "bz11", "bz20", "af1", "az3", "ay2", "uz1", "f0", "s0",
    "bz21", "af7", "ay6", "f1", "bz30", "s1", "af2", "m0", "az4", "ay3", "f7", "s7", "af6", "ay5", "m1", "p0", "bz31",
    "f2", "af3", "b0", "f6", "m7", "p1", "s2", "vz0", "s6", "af5", "ay4", "uz2", "b1", "bz4", "f3", "p7", "f5", "m2",
    "s3", "b7", "af4", "s5", "m6", "p2", "f4", "b2", "s4", "m3", "vz1", "m5", "vz3", "vz2", "p6", "b6", "m4", "vz4",
    "p3", "b3", "p5", "vx", "p4", "b5", "fin",
)


def gelu_pair(preact):
    tangent = jnp.tanh(gelu_coef * (preact + cubic_coef * preact * preact * preact))
    gelu_value = 0.5 * preact * (1.0 + tangent)
    gelu_slope = 0.5 * (1.0 + tangent) + 0.5 * preact * (1.0 - tangent * tangent) * gelu_coef * (
        1.0 + 3.0 * cubic_coef * preact * preact
    )
    return (gelu_value, gelu_slope)


def kernel(
    tok_hbm, w_hbm, up_hbm,
    act_hbm, grad_hbm, last_tok_hbm, last_grad_hbm,
    xa, xb, wv, acc, own, give, got, part, share, grads, up1, up2, val2, val1,
    send_sem, recv_sem, load_sem, store_sem, act_sem, last_sem,
):
    row, col, depth = lax.axis_index("row"), lax.axis_index("col"), lax.axis_index("depth")
    y, zlo = lax.rem(row, 4), row // 4
    z = col * 2 + zlo
    x, core = depth // 2, lax.rem(depth, 2)

    def at(y_, z_, x_, core_):
        return (lax.rem(z_, 2) * 4 + y_, z_ // 2, x_ * 2 + core_)

    def y_to(k):
        return at(lax.rem(y + k, 4), z, x, core)

    def z_to(k):
        return at(y, lax.rem(z + k, 8), x, core)

    def x_to(k):
        return at(y, z, lax.rem(x + k, 4), core)

    def col_to(k):
        return (row, lax.rem(col + k, 4), depth)

    partner = at(y, z, x, 1 - core)
    numbers = {}
    sent = {}

    def copy(name, src, dst, device):
        n = numbers.setdefault(name, len(numbers))
        return pltpu.make_async_remote_copy(
            src_ref=src, dst_ref=dst, send_sem=send_sem.at[n], recv_sem=recv_sem.at[n],
            device_id=device, device_id_type=MESH,
        )

    def send(name, src, dst, device):
        c = copy(name, src, dst, device)
        c.start()
        sent[name] = c

    def arrive(name, dst):
        copy(name, dst, dst, partner).wait_recv()

    mine = pl.ds(pl.multiple_of(core * HALF, 128), HALF)
    theirs = pl.ds(pl.multiple_of((1 - core) * HALF, 128), HALF)
    halves = ((mine, pl.ds(0, HALF)), (theirs, pl.ds(HALF, HALF)))
    loads = [
        pltpu.make_async_copy(tok_hbm.at[:, pl.ds(0, KA)], xa.at[0, pl.ds(0, TOK)], load_sem.at[0]),
        pltpu.make_async_copy(tok_hbm.at[:, pl.ds(KA, KB)], xb.at[0, pl.ds(0, TOK)], load_sem.at[1]),
    ]
    for i, (there, here) in enumerate(halves):
        loads.append(pltpu.make_async_copy(w_hbm.at[:, there], wv.at[:, here], load_sem.at[2 + i]))

    def home_row(x_of, x_home):
        return lax.rem(y + x_of + col + 4 - x_home, 4)

    loads.append(pltpu.make_async_copy(up_hbm.at[:, home_row(x, x)], up1.at[x], load_sem.at[4]))
    for c in loads:
        c.start()

    barrier = pltpu.get_barrier_semaphore()
    others = (
        [y_to(1), y_to(3), z_to(1), z_to(7), partner]
        + [x_to(k) for k in (1, 2, 3)]
    )
    for other in others:
        pl.semaphore_signal(barrier, inc=1, device_id=other, device_id_type=MESH)
    pl.semaphore_wait(barrier, len(others))

    LOW, HIGH = pl.ds(0, 32), pl.ds(32, 32)

    def rows(dy, lo=0, n=TOK):
        return pl.ds(dy * TOK + lo, n)

    def a_along_z(k):
        down, up = (k - 1) % 8, (1 - k) % 8
        if k < 4:
            send(("az-", k), xa.at[down, rows(0)], xa.at[k, rows(0)], z_to(7))
            send(("az+", k), xa.at[up, rows(0)], xa.at[8 - k, rows(0)], z_to(1))
        else:
            send(("az-", 4), xa.at[3, LOW], xa.at[4, LOW], z_to(7))
            send(("az+", 4), xa.at[5, HIGH], xa.at[4, HIGH], z_to(1))

    def a_from_z(k):
        if k < 4:
            arrive(("az-", k), xa.at[k, rows(0)])
            arrive(("az+", k), xa.at[8 - k, rows(0)])
        else:
            arrive(("az-", 4), xa.at[4, LOW])
            arrive(("az+", 4), xa.at[4, HIGH])

    def a_along_y(dz):
        send(("ay-", dz), xa.at[dz, rows(0)], xa.at[dz, rows(1)], y_to(3))
        send(("ay+", dz), xa.at[dz, rows(0)], xa.at[dz, rows(3)], y_to(1))

    def a_from_y(dz):
        arrive(("ay-", dz), xa.at[dz, rows(1)])
        arrive(("ay+", dz), xa.at[dz, rows(3)])

    def a_far_y(dz):
        send(("af-", dz), xa.at[dz, rows(1, 0, 32)], xa.at[dz, rows(2, 0, 32)], y_to(3))
        send(("af+", dz), xa.at[dz, rows(3, 32, 32)], xa.at[dz, rows(2, 32, 32)], y_to(1))

    def a_from_far(dz):
        arrive(("af-", dz), xa.at[dz, rows(2, 0, 32)])
        arrive(("af+", dz), xa.at[dz, rows(2, 32, 32)])

    def b_along_y():
        send("by-", xb.at[0, rows(0)], xb.at[0, rows(1)], y_to(3))
        send("by+", xb.at[0, rows(0)], xb.at[0, rows(3)], y_to(1))

    def b_from_y():
        arrive("by-", xb.at[0, rows(1)])
        arrive("by+", xb.at[0, rows(3)])

    def b_far_y():
        send("bf-", xb.at[0, rows(1, 0, 32)], xb.at[0, rows(2, 0, 32)], y_to(3))
        send("bf+", xb.at[0, rows(3, 32, 32)], xb.at[0, rows(2, 32, 32)], y_to(1))

    def b_from_far():
        arrive("bf-", xb.at[0, rows(2, 0, 32)])
        arrive("bf+", xb.at[0, rows(2, 32, 32)])

    HALVES = (pl.ds(0, 128), pl.ds(128, 128))

    def b_along_z(k, h):
        down, up, part_rows = (k - 1) % 8, (1 - k) % 8, HALVES[h]
        send(("bz-", k, h), xb.at[down, part_rows], xb.at[k, part_rows], z_to(7))
        send(("bz+", k, h), xb.at[up, part_rows], xb.at[8 - k, part_rows], z_to(1))

    def b_from_z(k, h):
        arrive(("bz-", k, h), xb.at[k, HALVES[h]])
        arrive(("bz+", k, h), xb.at[8 - k, HALVES[h]])

    def b_far_z():
        send("bq-", xb.at[3, HALVES[0]], xb.at[4, HALVES[0]], z_to(7))
        send("bq+", xb.at[5, HALVES[1]], xb.at[4, HALVES[1]], z_to(1))

    def b_from_far_z():
        arrive("bq-", xb.at[4, HALVES[0]])
        arrive("bq+", xb.at[4, HALVES[1]])

    def up_along_x():
        for k in (1, 2, 3):
            there = lax.rem(x + k, 4)
            send(("ux", k), up_hbm.at[:, home_row(there, x)], up1.at[x], x_to(k))

    def up_from_x():
        loads[4].wait()
        for k in (1, 2, 3):
            arrive(("ux", k), up1.at[lax.rem(x + 4 - k, 4)])

    stay = pltpu.make_async_copy(up1.at[col], up2.at[0], load_sem.at[5])

    def up_along_z(ks):
        for k in ks:
            send(("uz", k), up1.at[lax.rem(col + k, 4)], up2.at[4 - k], col_to(k))

    def up_from_z(ks):
        for k in ks:
            arrive(("uz", k), up2.at[4 - k])

    def act_along_z(delta):
        if delta == 0:
            pltpu.make_async_copy(val2.at[0], val1.at[col], act_sem.at[0]).start()
        else:
            send(("vz", delta), val2.at[delta], val1.at[col], col_to(delta))

    def act_half_along_z(odd, name):
        send((name, 2), val2.at[2, odd], val1.at[col, odd], col_to(2))

    def act_from_z(delta):
        arrive(("vz", delta), val1.at[lax.rem(col + 4 - delta, 4)])

    def act_half_from_z(odd, name):
        arrive((name, 2), val1.at[lax.rem(col + 2, 4), odd])

    def act_along_x():
        pltpu.make_async_copy(val2.at[0], val1.at[col], act_sem.at[0]).wait()
        for k in (1, 2, 3):
            there = lax.rem(x + k, 4)
            send(("vx", k), val1.at[there], act_hbm.at[:, home_row(x, there)], x_to(k))
        pltpu.make_async_copy(val1.at[x], act_hbm.at[:, home_row(x, x)], act_sem.at[1]).start()

    def act_done():
        pltpu.make_async_copy(val1.at[x], act_hbm.at[:, home_row(x, x)], act_sem.at[1]).wait()
        for k in (1, 2, 3):
            arrive(("vx", k), act_hbm.at[:, home_row(lax.rem(x + 4 - k, 4), x)])

    def delta_of(dz):
        return lax.rem((zlo + dz) // 2, 4)

    def chunk_rows(dz, x_of):
        dy = lax.rem(x_of + delta_of(dz), 4)
        return pl.ds(pl.multiple_of(dy * TOK, TOK), TOK)

    def forward(dz):
        for n in range(3):
            columns = pl.ds(n * 256, 256)
            value = jnp.dot(xa[dz], wv[pl.ds(0, KA), columns], preferred_element_type=jnp.float32)
            value = value + jnp.dot(xb[dz], wv[pl.ds(KA, KB), columns], preferred_element_type=jnp.float32)
            if n == 0:
                own[dz, :, pl.ds(0, 256)] = value
            elif n == 1:
                own[dz, :, pl.ds(256, 128)] = value[:, :128]
                give[dz, :, pl.ds(0, 128)] = value[:, 128:].astype(jnp.bfloat16)
            else:
                give[dz, :, pl.ds(128, 256)] = value.astype(jnp.bfloat16)
        send(("pair", dz), give.at[dz], got.at[dz], partner)

    def scatter(dz):
        total = own[dz] + got[dz].astype(jnp.float32)
        own[dz] = total
        part[dz] = total.astype(jnp.bfloat16)
        for k in (1, 2, 3):
            chunk = chunk_rows(dz, lax.rem(x + k, 4))
            send(("sum", dz, k), part.at[dz, chunk], share.at[dz, k - 1], x_to(k))

    def middle(dz):
        chunk = chunk_rows(dz, x)
        summed = own[dz, chunk, :]
        for k in range(3):
            summed = summed + share[dz, k].astype(jnp.float32)
        gelu_value, gelu_slope = gelu_pair(summed * fan_scale)
        delta, odd = delta_of(dz), lax.rem(zlo + dz, 2)
        val2[delta, odd] = gelu_value.astype(jnp.bfloat16)
        grads[dz, 0, chunk, :] = (up2[delta, odd].astype(jnp.float32) * gelu_slope).astype(jnp.bfloat16)
        for k in (1, 2, 3):
            send(("grad", dz, k), grads.at[dz, 0, chunk], grads.at[dz, 0, chunk], x_to(k))

    def pass_on(dz):
        send(("both", dz), grads.at[dz, 0], grads.at[dz, 1], partner)

    def gradient_tile(dz, tile):
        both = jnp.concatenate([grads[dz, 0], grads[dz, 1]], axis=1)
        if isinstance(tile, tuple):
            source, columns = tile
        return lax.dot_general(
            source[dz, :, columns], both, (((0,), (0,)), ((), ())), preferred_element_type=jnp.float32
        )

    TILE = 256
    begun = []

    def backward(dz):
        first = not begun
        begun.append(dz)
        last = len(begun) == 7

        for source, base, count in ((xa, 0, KA // TILE), (xb, KA, KB // TILE)):
            @pl.loop(0, count)
            def _(t):
                columns = pl.ds(pl.multiple_of(t * TILE, TILE), TILE)
                out = pl.ds(pl.multiple_of(base + t * TILE, TILE), TILE)
                value = gradient_tile(dz, (source, columns))
                acc[out, :] = value if first else acc[out, :] + value
                if last:
                    for c in stores(base // TILE + t):
                        c.start()

    def stores(tile):
        out = pl.ds(pl.multiple_of(tile * TILE, TILE), TILE)
        result = []
        for i, (there, here) in enumerate(halves):
            result.append(pltpu.make_async_copy(acc.at[out, here], grad_hbm.at[out, there], store_sem.at[tile, i]))
        return result

    last_tok = [
        pltpu.make_async_copy(xa.at[4], last_tok_hbm.at[:, pl.ds(0, KA)], last_sem.at[0]),
        pltpu.make_async_copy(xb.at[4], last_tok_hbm.at[:, pl.ds(KA, KB)], last_sem.at[1]),
    ]
    last_grad = [
        pltpu.make_async_copy(grads.at[4, 0], last_grad_hbm.at[:, mine], last_sem.at[2]),
        pltpu.make_async_copy(grads.at[4, 1], last_grad_hbm.at[:, theirs], last_sem.at[3]),
    ]

    def forward_last():
        forward(4)
        for c in last_tok:
            c.start()

    def finish():
        for c in last_grad:
            c.start()

    def sums_from(dz):
        for k in (1, 2, 3):
            arrive(("sum", dz, k), share.at[dz, k - 1])

    def grads_from(dz):
        for k in (1, 2, 3):
            arrive(("grad", dz, k), grads.at[dz, 0, chunk_rows(dz, lax.rem(x + 4 - k, 4))])

    def wait_all(copies):
        for c in copies:
            c.wait()

    received = {
        "tok_a": loads[0].wait, "tok_b": loads[1].wait, "by": b_from_y, "bf": b_from_far, "bz4": b_from_far_z,
        "ux": up_from_x, "uz0": stay.wait, "uz1": lambda: up_from_z((1, 3)), "uz2": lambda: up_from_z((2,)),
        "w": lambda: wait_all(loads[2:4]),
    }
    for k in (1, 2, 3, 4):
        received[f"az{k}"] = functools.partial(a_from_z, k)
        for h in (0, 1):
            received[f"bz{k}{h}"] = functools.partial(b_from_z, k, h)
    for dz in range(8):
        received[f"ay{dz}"] = functools.partial(a_from_y, dz)
        received[f"af{dz}"] = functools.partial(a_from_far, dz)
        received[f"pair{dz}"] = functools.partial(lambda d: arrive(("pair", d), got.at[d]), dz)
        received[f"sum{dz}"] = functools.partial(sums_from, dz)
        received[f"grad{dz}"] = functools.partial(grads_from, dz)
        received[f"both{dz}"] = functools.partial(lambda d: arrive(("both", d), grads.at[d, 1]), dz)
    for delta in (1, 2, 3):
        received[f"vz{delta}"] = functools.partial(act_from_z, delta)

    def begin():
        need("tok_a")
        a_along_z(1)
        need("tok_b")
        b_along_y()
        a_along_y(0)
        up_along_x()

    events = {
        "start": ((), begin),
        "bfar": (("by",), b_far_y),
        "bz4": (("bz30", "bz31"), b_far_z),
        "u0": (("ux",), stay.start),
        "uz1": (("ux", "az2"), lambda: up_along_z((1, 3))),
        "uz2": (("ux", "az4"), lambda: up_along_z((2,))),
        "vx": (("vz1", "vz2", "vz3", "vz4"), act_along_x),
        "fin": (("both4",), finish),
    }
    for k in (2, 3, 4):
        events[f"az{k}"] = ((f"az{k - 1}",), functools.partial(a_along_z, k))
    for h in (0, 1):
        events[f"bz1{h}"] = (("by", "bf") if h else ("by",), functools.partial(b_along_z, 1, h))
        for k in (2, 3):
            events[f"bz{k}{h}"] = ((f"bz{k - 1}{h}",), functools.partial(b_along_z, k, h))
    for dz in range(8):
        k = min(dz, 8 - dz)
        lower = {0: ("by", "bf"), 4: ("bz4",)}.get(k, (f"bz{k}0", f"bz{k}1"))
        upper = {0: ("uz0",), 1: ("uz0", "uz1"), 2: ("uz1",), 3: ("uz1", "uz2"), 4: ("uz2",)}[k]
        if dz:
            events[f"ay{dz}"] = ((f"az{k}",), functools.partial(a_along_y, dz))
        events[f"af{dz}"] = ((f"ay{dz}",), functools.partial(a_far_y, dz))
        events[f"f{dz}"] = (("w", f"af{dz}") + lower, functools.partial(forward, dz))
        events[f"s{dz}"] = ((f"pair{dz}",), functools.partial(scatter, dz))
        events[f"m{dz}"] = ((f"sum{dz}",) + upper, functools.partial(middle, dz))
        events[f"p{dz}"] = ((f"grad{dz}",), functools.partial(pass_on, dz))
        events[f"b{dz}"] = ((f"both{dz}",), functools.partial(backward, dz))
    events["f4"] = (events["f4"][0], forward_last)
    for delta in range(4):
        events[f"vz{delta}"] = ((), functools.partial(act_along_z, delta))
    events["vz2"] = ((), functools.partial(act_half_along_z, 1 - zlo, "va"))
    events["vz4"] = ((), functools.partial(act_half_along_z, zlo, "vb"))
    received["vz2"] = functools.partial(act_half_from_z, 1 - zlo, "va")
    received["vz4"] = functools.partial(act_half_from_z, zlo, "vb")

    had = set()

    def need(name):
        if name not in had:
            had.add(name)
            received[name]()

    for name in ORDER:
        needs, do = events[name]
        for other in needs:
            need(other)
        do()
    act_done()
    for tile in range(FEAT // TILE):
        for c in stores(tile):
            c.wait()
    for c in last_tok + last_grad:
        c.wait()
    for c in sent.values():
        c.wait_send()
    assert len(numbers) <= NSEM, len(numbers)


def update(act_in, tok_ref, grad_ref, sum_ref, w_ref, m_ref, act_out, nw_ref, nm_ref, act_sem):
    step = pl.program_id(0)
    act = pltpu.make_async_copy(act_in, act_out, act_sem)

    @pl.when(step == 0)
    def _():
        act.start()

    grad_sum = sum_ref[...] + lax.dot_general(
        tok_ref[...], grad_ref[...], (((0,), (0,)), ((), ())), preferred_element_type=jnp.float32
    )
    moment_f = m_ref[...].astype(jnp.float32)
    weight_f = w_ref[...].astype(jnp.float32)
    blended = beta_one * moment_f + ((1.0 - beta_one) * fan_scale) * grad_sum
    sign = blended * lax.rsqrt(blended * blended + smooth_tau * smooth_tau)
    nw_ref[...] = ((1.0 - lion_rate * decay_rate) * weight_f - lion_rate * sign).astype(jnp.bfloat16)
    nm_ref[...] = (beta_two * moment_f + ((1.0 - beta_two) * fan_scale) * grad_sum).astype(jnp.bfloat16)

    @pl.when(step == pl.num_programs(0) - 1)
    def _():
        act.wait()


def shards(tokens, weight, moment, upstream):
    bf16, f32 = jnp.bfloat16, jnp.float32
    any_space = pl.BlockSpec(memory_space=pl.ANY)
    act_shape = jax.ShapeDtypeStruct((2, 4, TOK, HALF), bf16)
    block_shape = jax.ShapeDtypeStruct((FEAT, HID), bf16)
    act, grad_sum, last_tok, last_grad = pl.pallas_call(
        kernel,
        out_shape=(
            act_shape,
            jax.ShapeDtypeStruct((FEAT, HID), f32),
            jax.ShapeDtypeStruct((PIECE, FEAT), bf16),
            jax.ShapeDtypeStruct((PIECE, HID), bf16),
        ),
        in_specs=[any_space] * 3,
        out_specs=(any_space,) * 4,
        scratch_shapes=[
            pltpu.VMEM((8, PIECE, KA), bf16),
            pltpu.VMEM((8, PIECE, KB), bf16),
            pltpu.VMEM((FEAT, HID), bf16),
            pltpu.VMEM((FEAT, HID), f32),
            pltpu.VMEM((8, PIECE, HALF), f32),
            pltpu.VMEM((8, PIECE, HALF), bf16),
            pltpu.VMEM((8, PIECE, HALF), bf16),
            pltpu.VMEM((8, PIECE, HALF), bf16),
            pltpu.VMEM((8, 3, TOK, HALF), bf16),
            pltpu.VMEM((8, 2, PIECE, HALF), bf16),
            pltpu.VMEM((4, 2, TOK, HALF), bf16),
            pltpu.VMEM((4, 2, TOK, HALF), bf16),
            pltpu.VMEM((4, 2, TOK, HALF), bf16),
            pltpu.VMEM((4, 2, TOK, HALF), bf16),
            pltpu.SemaphoreType.DMA((NSEM,)),
            pltpu.SemaphoreType.DMA((NSEM,)),
            pltpu.SemaphoreType.DMA((6,)),
            pltpu.SemaphoreType.DMA((FEAT // 256, 2)),
            pltpu.SemaphoreType.DMA((2,)),
            pltpu.SemaphoreType.DMA((4,)),
        ],
        compiler_params=pltpu.CompilerParams(
            collective_id=0, has_side_effects=True, vmem_limit_bytes=58 * 1024 * 1024
        ),
        cost_estimate=pl.CostEstimate(
            flops=4 * 2048 * FEAT * HID, bytes_accessed=12 * 1024 * 1024, transcendentals=2 * FEAT * HID
        ),
    )(tokens, weight, upstream.reshape(2, 4, TOK, HALF))
    tile = pl.BlockSpec((UPDATE, HID), lambda t: (t, 0))
    act, new_weight, new_moment = pl.pallas_call(
        update,
        out_shape=(act_shape, block_shape, block_shape),
        grid=(FEAT // UPDATE,),
        in_specs=[
            any_space,
            pl.BlockSpec((PIECE, UPDATE), lambda t: (0, t)),
            pl.BlockSpec((PIECE, HID), lambda t: (0, 0)),
            tile,
            tile,
            tile,
        ],
        out_specs=(any_space, tile, tile),
        scratch_shapes=[pltpu.SemaphoreType.DMA],
        compiler_params=pltpu.CompilerParams(vmem_limit_bytes=24 * 1024 * 1024),
        cost_estimate=pl.CostEstimate(
            flops=2 * PIECE * FEAT * HID, bytes_accessed=16 * FEAT * HID, transcendentals=FEAT * HID
        ),
    )(act, last_tok, last_grad, grad_sum, weight, moment)
    return (act.reshape(upstream.shape), new_weight, new_moment)


def solution(mesh):
    placed = (
        P(("row", "col"), "depth"),
        P("depth", ("row", "col")),
        P("depth", ("row", "col")),
        P(None, "col", ("row", "depth")),
    )
    return jax.shard_map(
        shards,
        mesh=mesh,
        in_specs=placed,
        out_specs=(
            P(None, "col", ("row", "depth")),
            P("depth", ("row", "col")),
            P("depth", ("row", "col")),
        ),
        check_vma=False,
    )
```

```python
import functools

import jax
import jax.numpy as jnp
from jax import lax
from jax.experimental import pallas as pl
from jax.experimental.pallas import tpu as pltpu
from jax.sharding import PartitionSpec as P

D = 12288
TOK = 64
KA = 1024
KB = 512
FEAT = 1536
HID = 768
HALF = 384
PIECE = 256
NSEM = 176
UPDATE = 256

gelu_coef = 0.7978845608028654
cubic_coef = 0.044715
lion_rate = 0.5
decay_rate = 0.1
beta_one = 0.9
beta_two = 0.99
smooth_tau = 0.1
fan_scale = D ** (-0.5)

MESH = pl.DeviceIdType.MESH

ORDER = (
    "start", "bz10", "bfar", "ay1", "az2", "af0", "ay7", "u0", "bz11", "bz20", "af1", "ay2", "az3", "uz1", "f0", "s0",
    "bz21", "af7", "ay6", "f1", "bz30", "s1", "af2", "m0", "az4", "ay3", "f7", "s7", "af6", "ay5", "r0", "m1", "f2",
    "m7", "af3", "p0", "vz0", "bz31", "r1", "f6", "s2", "b0", "s6", "af5", "ay4", "r7", "p1", "uz2", "b1", "bz4",
    "f3", "m2", "f5", "m6", "p7", "s3", "af4", "s5", "r2", "b7", "r6", "f4", "m3", "vz1", "s4", "m5", "vz3", "p2",
    "vz2", "p6", "r3", "b2", "b6", "m4", "vz4", "r5", "p3", "vp", "b3", "r4", "p5", "vq", "b5", "p4", "fin",
)


def gelu_pair(preact):
    tangent = jnp.tanh(gelu_coef * (preact + cubic_coef * preact * preact * preact))
    gelu_value = 0.5 * preact * (1.0 + tangent)
    gelu_slope = 0.5 * (1.0 + tangent) + 0.5 * preact * (1.0 - tangent * tangent) * gelu_coef * (
        1.0 + 3.0 * cubic_coef * preact * preact
    )
    return (gelu_value, gelu_slope)


def kernel(
    tok_hbm, w_hbm, up_hbm,
    act_hbm, grad_hbm, last_tok_hbm, last_grad_hbm,
    xa, xb, wv, acc, own, give, got, part, share, grads, up1, up2, val2, val1,
    send_sem, recv_sem, load_sem, store_sem, act_sem, last_sem,
):
    row, col, depth = lax.axis_index("row"), lax.axis_index("col"), lax.axis_index("depth")
    y, zlo = lax.rem(row, 4), row // 4
    z = col * 2 + zlo
    x, core = depth // 2, lax.rem(depth, 2)

    def at(y_, z_, x_, core_):
        return (lax.rem(z_, 2) * 4 + y_, z_ // 2, x_ * 2 + core_)

    def y_to(k):
        return at(lax.rem(y + k, 4), z, x, core)

    def z_to(k):
        return at(y, lax.rem(z + k, 8), x, core)

    def x_to(k):
        return at(y, z, lax.rem(x + k, 4), core)

    def col_to(k):
        return (row, lax.rem(col + k, 4), depth)

    partner = at(y, z, x, 1 - core)
    numbers = {}
    sent = {}

    def copy(name, src, dst, device):
        n = numbers.setdefault(name, len(numbers))
        return pltpu.make_async_remote_copy(
            src_ref=src, dst_ref=dst, send_sem=send_sem.at[n], recv_sem=recv_sem.at[n],
            device_id=device, device_id_type=MESH,
        )

    def send(name, src, dst, device):
        c = copy(name, src, dst, device)
        c.start()
        sent[name] = c

    def arrive(name, dst):
        copy(name, dst, dst, partner).wait_recv()

    mine = pl.ds(pl.multiple_of(core * HALF, 128), HALF)
    theirs = pl.ds(pl.multiple_of((1 - core) * HALF, 128), HALF)
    halves = ((mine, pl.ds(0, HALF)), (theirs, pl.ds(HALF, HALF)))
    loads = [
        pltpu.make_async_copy(tok_hbm.at[:, pl.ds(0, KA)], xa.at[0, pl.ds(0, TOK)], load_sem.at[0]),
        pltpu.make_async_copy(tok_hbm.at[:, pl.ds(KA, KB)], xb.at[0, pl.ds(0, TOK)], load_sem.at[1]),
    ]
    for i, (there, here) in enumerate(halves):
        loads.append(pltpu.make_async_copy(w_hbm.at[:, there], wv.at[:, here], load_sem.at[2 + i]))

    def home_row(x_of, x_home):
        return lax.rem(y + x_of + col + 4 - x_home, 4)

    loads.append(pltpu.make_async_copy(up_hbm.at[:, home_row(x, x)], up1.at[x], load_sem.at[4]))
    for c in loads:
        c.start()

    barrier = pltpu.get_barrier_semaphore()
    others = (
        [y_to(1), y_to(3), z_to(1), z_to(7), partner]
        + [x_to(k) for k in (1, 2, 3)]
    )
    for other in others:
        pl.semaphore_signal(barrier, inc=1, device_id=other, device_id_type=MESH)
    pl.semaphore_wait(barrier, len(others))

    LOW, HIGH = pl.ds(0, 32), pl.ds(32, 32)

    def rows(dy, lo=0, n=TOK):
        return pl.ds(dy * TOK + lo, n)

    def a_along_z(k):
        down, up = (k - 1) % 8, (1 - k) % 8
        if k < 4:
            send(("az-", k), xa.at[down, rows(0)], xa.at[k, rows(0)], z_to(7))
            send(("az+", k), xa.at[up, rows(0)], xa.at[8 - k, rows(0)], z_to(1))
        else:
            send(("az-", 4), xa.at[3, LOW], xa.at[4, LOW], z_to(7))
            send(("az+", 4), xa.at[5, HIGH], xa.at[4, HIGH], z_to(1))

    def a_from_z(k):
        if k < 4:
            arrive(("az-", k), xa.at[k, rows(0)])
            arrive(("az+", k), xa.at[8 - k, rows(0)])
        else:
            arrive(("az-", 4), xa.at[4, LOW])
            arrive(("az+", 4), xa.at[4, HIGH])

    def a_along_y(dz):
        send(("ay-", dz), xa.at[dz, rows(0)], xa.at[dz, rows(1)], y_to(3))
        send(("ay+", dz), xa.at[dz, rows(0)], xa.at[dz, rows(3)], y_to(1))

    def a_from_y(dz):
        arrive(("ay-", dz), xa.at[dz, rows(1)])
        arrive(("ay+", dz), xa.at[dz, rows(3)])

    def a_far_y(dz):
        send(("af-", dz), xa.at[dz, rows(1, 0, 32)], xa.at[dz, rows(2, 0, 32)], y_to(3))
        send(("af+", dz), xa.at[dz, rows(3, 32, 32)], xa.at[dz, rows(2, 32, 32)], y_to(1))

    def a_from_far(dz):
        arrive(("af-", dz), xa.at[dz, rows(2, 0, 32)])
        arrive(("af+", dz), xa.at[dz, rows(2, 32, 32)])

    def b_along_y():
        send("by-", xb.at[0, rows(0)], xb.at[0, rows(1)], y_to(3))
        send("by+", xb.at[0, rows(0)], xb.at[0, rows(3)], y_to(1))

    def b_from_y():
        arrive("by-", xb.at[0, rows(1)])
        arrive("by+", xb.at[0, rows(3)])

    def b_far_y():
        send("bf-", xb.at[0, rows(1, 0, 32)], xb.at[0, rows(2, 0, 32)], y_to(3))
        send("bf+", xb.at[0, rows(3, 32, 32)], xb.at[0, rows(2, 32, 32)], y_to(1))

    def b_from_far():
        arrive("bf-", xb.at[0, rows(2, 0, 32)])
        arrive("bf+", xb.at[0, rows(2, 32, 32)])

    HALVES = (pl.ds(0, 128), pl.ds(128, 128))

    def b_along_z(k, h):
        down, up, part_rows = (k - 1) % 8, (1 - k) % 8, HALVES[h]
        send(("bz-", k, h), xb.at[down, part_rows], xb.at[k, part_rows], z_to(7))
        send(("bz+", k, h), xb.at[up, part_rows], xb.at[8 - k, part_rows], z_to(1))

    def b_from_z(k, h):
        arrive(("bz-", k, h), xb.at[k, HALVES[h]])
        arrive(("bz+", k, h), xb.at[8 - k, HALVES[h]])

    def b_far_z():
        send("bq-", xb.at[3, HALVES[0]], xb.at[4, HALVES[0]], z_to(7))
        send("bq+", xb.at[5, HALVES[1]], xb.at[4, HALVES[1]], z_to(1))

    def b_from_far_z():
        arrive("bq-", xb.at[4, HALVES[0]])
        arrive("bq+", xb.at[4, HALVES[1]])

    def up_along_x():
        for k in (1, 2, 3):
            there = lax.rem(x + k, 4)
            send(("ux", k), up_hbm.at[:, home_row(there, x)], up1.at[x], x_to(k))

    def up_from_x():
        loads[4].wait()
        for k in (1, 2, 3):
            arrive(("ux", k), up1.at[lax.rem(x + 4 - k, 4)])

    stay = pltpu.make_async_copy(up1.at[col], up2.at[0], load_sem.at[5])

    def up_along_z(ks):
        for k in ks:
            send(("uz", k), up1.at[lax.rem(col + k, 4)], up2.at[4 - k], col_to(k))

    def up_from_z(ks):
        for k in ks:
            arrive(("uz", k), up2.at[4 - k])

    def act_along_z(delta):
        if delta == 0:
            act_stay.start()
        else:
            send(("vz", delta), val2.at[delta], val1.at[col], col_to(delta))

    def act_half_along_z(odd, name):
        send((name, 2), val2.at[2, odd], val1.at[col, odd], col_to(2))

    def act_from_z(delta):
        arrive(("vz", delta), val1.at[lax.rem(col + 4 - delta, 4)])

    def act_half_from_z(odd, name):
        arrive((name, 2), val1.at[lax.rem(col + 2, 4), odd])

    def act_along_x(odd, name):
        for k in (1, 2, 3):
            there = lax.rem(x + k, 4)
            send((name, k), val1.at[there, odd], act_hbm.at[odd, home_row(x, there)], x_to(k))

    act_stay = pltpu.make_async_copy(val2.at[0], val1.at[col], act_sem.at[0])
    act_here = pltpu.make_async_copy(val1.at[x], act_hbm.at[:, home_row(x, x)], act_sem.at[1])

    def act_late():
        act_along_x(zlo, "vq")
        act_here.start()

    def act_done():
        act_here.wait()
        for odd, name in ((1 - zlo, "vp"), (zlo, "vq")):
            for k in (1, 2, 3):
                arrive((name, k), act_hbm.at[odd, home_row(lax.rem(x + 4 - k, 4), x)])

    def delta_of(dz):
        return lax.rem((zlo + dz) // 2, 4)

    def chunk_rows(dz, x_of):
        dy = lax.rem(x_of + delta_of(dz), 4)
        return pl.ds(pl.multiple_of(dy * TOK, TOK), TOK)

    def forward(dz):
        for n in range(3):
            columns = pl.ds(n * 256, 256)
            value = jnp.dot(xa[dz], wv[pl.ds(0, KA), columns], preferred_element_type=jnp.float32)
            value = value + jnp.dot(xb[dz], wv[pl.ds(KA, KB), columns], preferred_element_type=jnp.float32)
            if n == 0:
                own[dz, :, pl.ds(0, 256)] = value
            elif n == 1:
                own[dz, :, pl.ds(256, 128)] = value[:, :128]
                give[dz, :, pl.ds(0, 128)] = value[:, 128:].astype(jnp.bfloat16)
            else:
                give[dz, :, pl.ds(128, 256)] = value.astype(jnp.bfloat16)
        send(("pair", dz), give.at[dz], got.at[dz], partner)

    def scatter(dz):
        total = own[dz] + got[dz].astype(jnp.float32)
        own[dz] = total
        part[dz] = total.astype(jnp.bfloat16)
        for k in (1, 2, 3):
            chunk = chunk_rows(dz, lax.rem(x + k, 4))
            send(("sum", dz, k), part.at[dz, chunk], share.at[dz, k - 1], x_to(k))

    def middle(dz):
        chunk = chunk_rows(dz, x)
        summed = own[dz, chunk, :]
        for k in range(3):
            summed = summed + share[dz, k].astype(jnp.float32)
        gelu_value, gelu_slope = gelu_pair(summed * fan_scale)
        delta, odd = delta_of(dz), lax.rem(zlo + dz, 2)
        val2[delta, odd] = gelu_value.astype(jnp.bfloat16)
        grads[dz, 0, chunk, :] = (up2[delta, odd].astype(jnp.float32) * gelu_slope).astype(jnp.bfloat16)
        for k in (1, 3):
            send(("grad", dz, k), grads.at[dz, 0, chunk], grads.at[dz, 0, chunk], x_to(k))

    def half_chunk(dz, x_of, lo):
        dy = lax.rem(x_of + delta_of(dz), 4)
        return pl.ds(pl.multiple_of(dy * TOK + lo, 32), 32)

    def relay(dz):
        low, high = half_chunk(dz, lax.rem(x + 3, 4), 0), half_chunk(dz, lax.rem(x + 1, 4), 32)
        send(("far", dz, 1), grads.at[dz, 0, low], grads.at[dz, 0, low], x_to(1))
        send(("far", dz, 3), grads.at[dz, 0, high], grads.at[dz, 0, high], x_to(3))

    def far_from(dz):
        far = lax.rem(x + 2, 4)
        arrive(("far", dz, 1), grads.at[dz, 0, half_chunk(dz, far, 0)])
        arrive(("far", dz, 3), grads.at[dz, 0, half_chunk(dz, far, 32)])

    def pass_on(dz):
        send(("both", dz), grads.at[dz, 0], grads.at[dz, 1], partner)

    def gradient_tile(dz, tile):
        both = jnp.concatenate([grads[dz, 0], grads[dz, 1]], axis=1)
        if isinstance(tile, tuple):
            source, columns = tile
        return lax.dot_general(
            source[dz, :, columns], both, (((0,), (0,)), ((), ())), preferred_element_type=jnp.float32
        )

    TILE = 256
    begun = []

    def backward(dz):
        first = not begun
        begun.append(dz)
        last = len(begun) == 7

        for source, base, count in ((xa, 0, KA // TILE), (xb, KA, KB // TILE)):
            @pl.loop(0, count)
            def _(t):
                columns = pl.ds(pl.multiple_of(t * TILE, TILE), TILE)
                out = pl.ds(pl.multiple_of(base + t * TILE, TILE), TILE)
                value = gradient_tile(dz, (source, columns))
                acc[out, :] = value if first else acc[out, :] + value
                if last:
                    for c in stores(base // TILE + t):
                        c.start()

    def stores(tile):
        out = pl.ds(pl.multiple_of(tile * TILE, TILE), TILE)
        result = []
        for i, (there, here) in enumerate(halves):
            result.append(pltpu.make_async_copy(acc.at[out, here], grad_hbm.at[out, there], store_sem.at[tile, i]))
        return result

    last_tok = [
        pltpu.make_async_copy(xa.at[4], last_tok_hbm.at[:, pl.ds(0, KA)], last_sem.at[0]),
        pltpu.make_async_copy(xb.at[4], last_tok_hbm.at[:, pl.ds(KA, KB)], last_sem.at[1]),
    ]
    last_grad = [
        pltpu.make_async_copy(grads.at[4, 0], last_grad_hbm.at[:, mine], last_sem.at[2]),
        pltpu.make_async_copy(grads.at[4, 1], last_grad_hbm.at[:, theirs], last_sem.at[3]),
    ]

    def forward_last():
        forward(4)
        for c in last_tok:
            c.start()

    def finish():
        for c in last_grad:
            c.start()

    def sums_from(dz):
        for k in (1, 2, 3):
            arrive(("sum", dz, k), share.at[dz, k - 1])

    def grads_from(dz):
        for k in (1, 3):
            arrive(("grad", dz, k), grads.at[dz, 0, chunk_rows(dz, lax.rem(x + 4 - k, 4))])

    def wait_all(copies):
        for c in copies:
            c.wait()

    received = {
        "tok_a": loads[0].wait, "tok_b": loads[1].wait, "by": b_from_y, "bf": b_from_far, "bz4": b_from_far_z,
        "ux": up_from_x, "uz0": stay.wait, "uz1": lambda: up_from_z((1, 3)), "uz2": lambda: up_from_z((2,)),
        "w": lambda: wait_all(loads[2:4]),
    }
    for k in (1, 2, 3, 4):
        received[f"az{k}"] = functools.partial(a_from_z, k)
        for h in (0, 1):
            received[f"bz{k}{h}"] = functools.partial(b_from_z, k, h)
    for dz in range(8):
        received[f"ay{dz}"] = functools.partial(a_from_y, dz)
        received[f"af{dz}"] = functools.partial(a_from_far, dz)
        received[f"pair{dz}"] = functools.partial(lambda d: arrive(("pair", d), got.at[d]), dz)
        received[f"sum{dz}"] = functools.partial(sums_from, dz)
        received[f"near{dz}"] = functools.partial(grads_from, dz)
        received[f"grad{dz}"] = functools.partial(far_from, dz)
        received[f"both{dz}"] = functools.partial(lambda d: arrive(("both", d), grads.at[d, 1]), dz)
    for delta in (1, 2, 3):
        received[f"vz{delta}"] = functools.partial(act_from_z, delta)

    def begin():
        need("tok_a")
        a_along_z(1)
        need("tok_b")
        b_along_y()
        a_along_y(0)
        up_along_x()

    events = {
        "start": ((), begin),
        "bfar": (("by",), b_far_y),
        "bz4": (("bz30", "bz31"), b_far_z),
        "u0": (("ux",), stay.start),
        "uz1": (("ux", "az2"), lambda: up_along_z((1, 3))),
        "uz2": (("ux", "az4"), lambda: up_along_z((2,))),
        "vp": (("vz0", "vz1", "vz2", "vz3"), lambda: act_along_x(1 - zlo, "vp")),
        "vq": (("vz4",), act_late),
        "fin": (("both4",), finish),
    }
    for k in (2, 3, 4):
        events[f"az{k}"] = ((f"az{k - 1}",), functools.partial(a_along_z, k))
    for h in (0, 1):
        events[f"bz1{h}"] = (("by", "bf") if h else ("by",), functools.partial(b_along_z, 1, h))
        for k in (2, 3):
            events[f"bz{k}{h}"] = ((f"bz{k - 1}{h}",), functools.partial(b_along_z, k, h))
    for dz in range(8):
        k = min(dz, 8 - dz)
        lower = {0: ("by", "bf"), 4: ("bz4",)}.get(k, (f"bz{k}0", f"bz{k}1"))
        upper = {0: ("uz0",), 1: ("uz0", "uz1"), 2: ("uz1",), 3: ("uz1", "uz2"), 4: ("uz2",)}[k]
        if dz:
            events[f"ay{dz}"] = ((f"az{k}",), functools.partial(a_along_y, dz))
        events[f"af{dz}"] = ((f"ay{dz}",), functools.partial(a_far_y, dz))
        events[f"f{dz}"] = (("w", f"af{dz}") + lower, functools.partial(forward, dz))
        events[f"s{dz}"] = ((f"pair{dz}",), functools.partial(scatter, dz))
        events[f"m{dz}"] = ((f"sum{dz}",) + upper, functools.partial(middle, dz))
        events[f"r{dz}"] = ((f"near{dz}",), functools.partial(relay, dz))
        events[f"p{dz}"] = ((f"grad{dz}",), functools.partial(pass_on, dz))
        events[f"b{dz}"] = ((f"both{dz}",), functools.partial(backward, dz))
    events["f4"] = (events["f4"][0], forward_last)
    for delta in range(4):
        events[f"vz{delta}"] = ((), functools.partial(act_along_z, delta))
    events["vz2"] = ((), functools.partial(act_half_along_z, 1 - zlo, "va"))
    events["vz4"] = ((), functools.partial(act_half_along_z, zlo, "vb"))
    received["vz0"] = act_stay.wait
    received["vz2"] = functools.partial(act_half_from_z, 1 - zlo, "va")
    received["vz4"] = functools.partial(act_half_from_z, zlo, "vb")

    had = set()

    def need(name):
        if name not in had:
            had.add(name)
            received[name]()

    for name in ORDER:
        needs, do = events[name]
        for other in needs:
            need(other)
        do()
    act_done()
    for tile in range(FEAT // TILE):
        for c in stores(tile):
            c.wait()
    for c in last_tok + last_grad:
        c.wait()
    for c in sent.values():
        c.wait_send()
    assert len(numbers) <= NSEM, len(numbers)


def update(act_in, tok_ref, grad_ref, sum_ref, w_ref, m_ref, act_out, nw_ref, nm_ref, act_sem):
    step = pl.program_id(0)
    act = pltpu.make_async_copy(act_in, act_out, act_sem)

    @pl.when(step == 0)
    def _():
        act.start()

    grad_sum = sum_ref[...] + lax.dot_general(
        tok_ref[...], grad_ref[...], (((0,), (0,)), ((), ())), preferred_element_type=jnp.float32
    )
    moment_f = m_ref[...].astype(jnp.float32)
    weight_f = w_ref[...].astype(jnp.float32)
    blended = beta_one * moment_f + ((1.0 - beta_one) * fan_scale) * grad_sum
    sign = blended * lax.rsqrt(blended * blended + smooth_tau * smooth_tau)
    nw_ref[...] = ((1.0 - lion_rate * decay_rate) * weight_f - lion_rate * sign).astype(jnp.bfloat16)
    nm_ref[...] = (beta_two * moment_f + ((1.0 - beta_two) * fan_scale) * grad_sum).astype(jnp.bfloat16)

    @pl.when(step == pl.num_programs(0) - 1)
    def _():
        act.wait()


def shards(tokens, weight, moment, upstream):
    bf16, f32 = jnp.bfloat16, jnp.float32
    any_space = pl.BlockSpec(memory_space=pl.ANY)
    act_shape = jax.ShapeDtypeStruct((2, 4, TOK, HALF), bf16)
    block_shape = jax.ShapeDtypeStruct((FEAT, HID), bf16)
    act, grad_sum, last_tok, last_grad = pl.pallas_call(
        kernel,
        out_shape=(
            act_shape,
            jax.ShapeDtypeStruct((FEAT, HID), f32),
            jax.ShapeDtypeStruct((PIECE, FEAT), bf16),
            jax.ShapeDtypeStruct((PIECE, HID), bf16),
        ),
        in_specs=[any_space] * 3,
        out_specs=(any_space,) * 4,
        scratch_shapes=[
            pltpu.VMEM((8, PIECE, KA), bf16),
            pltpu.VMEM((8, PIECE, KB), bf16),
            pltpu.VMEM((FEAT, HID), bf16),
            pltpu.VMEM((FEAT, HID), f32),
            pltpu.VMEM((8, PIECE, HALF), f32),
            pltpu.VMEM((8, PIECE, HALF), bf16),
            pltpu.VMEM((8, PIECE, HALF), bf16),
            pltpu.VMEM((8, PIECE, HALF), bf16),
            pltpu.VMEM((8, 3, TOK, HALF), bf16),
            pltpu.VMEM((8, 2, PIECE, HALF), bf16),
            pltpu.VMEM((4, 2, TOK, HALF), bf16),
            pltpu.VMEM((4, 2, TOK, HALF), bf16),
            pltpu.VMEM((4, 2, TOK, HALF), bf16),
            pltpu.VMEM((4, 2, TOK, HALF), bf16),
            pltpu.SemaphoreType.DMA((NSEM,)),
            pltpu.SemaphoreType.DMA((NSEM,)),
            pltpu.SemaphoreType.DMA((6,)),
            pltpu.SemaphoreType.DMA((FEAT // 256, 2)),
            pltpu.SemaphoreType.DMA((2,)),
            pltpu.SemaphoreType.DMA((4,)),
        ],
        compiler_params=pltpu.CompilerParams(
            collective_id=0, has_side_effects=True, vmem_limit_bytes=58 * 1024 * 1024
        ),
        cost_estimate=pl.CostEstimate(
            flops=4 * 2048 * FEAT * HID, bytes_accessed=12 * 1024 * 1024, transcendentals=2 * FEAT * HID
        ),
    )(tokens, weight, upstream.reshape(2, 4, TOK, HALF))
    tile = pl.BlockSpec((UPDATE, HID), lambda t: (t, 0))
    act, new_weight, new_moment = pl.pallas_call(
        update,
        out_shape=(act_shape, block_shape, block_shape),
        grid=(FEAT // UPDATE,),
        in_specs=[
            any_space,
            pl.BlockSpec((PIECE, UPDATE), lambda t: (0, t)),
            pl.BlockSpec((PIECE, HID), lambda t: (0, 0)),
            tile,
            tile,
            tile,
        ],
        out_specs=(any_space, tile, tile),
        scratch_shapes=[pltpu.SemaphoreType.DMA],
        compiler_params=pltpu.CompilerParams(vmem_limit_bytes=58 * 1024 * 1024),
        cost_estimate=pl.CostEstimate(
            flops=2 * PIECE * FEAT * HID, bytes_accessed=16 * FEAT * HID, transcendentals=FEAT * HID
        ),
    )(act, last_tok, last_grad, grad_sum, weight, moment)
    return (act.reshape(upstream.shape), new_weight, new_moment)


def solution(mesh):
    placed = (
        P(("row", "col"), "depth"),
        P("depth", ("row", "col")),
        P("depth", ("row", "col")),
        P(None, "col", ("row", "depth")),
    )
    return jax.shard_map(
        shards,
        mesh=mesh,
        in_specs=placed,
        out_specs=(
            P(None, "col", ("row", "depth")),
            P("depth", ("row", "col")),
            P("depth", ("row", "col")),
        ),
        check_vma=False,
    )
```

```python
import functools

import jax
import jax.numpy as jnp
from jax import lax
from jax.experimental import pallas as pl
from jax.experimental.pallas import tpu as pltpu
from jax.sharding import PartitionSpec as P

D = 12288
TOK = 64
KA = 1024
KB = 512
FEAT = 1536
HID = 768
HALF = 384
PIECE = 256
NSEM = 176
UPDATE = 256

gelu_coef = 0.7978845608028654
cubic_coef = 0.044715
lion_rate = 0.5
decay_rate = 0.1
beta_one = 0.9
beta_two = 0.99
smooth_tau = 0.1
fan_scale = D ** (-0.5)

MESH = pl.DeviceIdType.MESH

ORDER = (
    "start", "bz10", "bfar", "ay1", "az2", "af0", "ay7", "u0", "bz11", "bz20", "af1", "ay2", "az3", "uz1", "f0", "s0",
    "bz21", "af7", "ay6", "f1", "bz30", "s1", "af2", "m0", "az4", "ay3", "f7", "s7", "af6", "ay5", "r0", "m1", "f2",
    "m7", "af3", "p0", "vz0", "bz31", "r1", "f6", "s2", "b0", "s6", "af5", "ay4", "r7", "p1", "uz2", "b1", "bz4",
    "f3", "m2", "f5", "m6", "p7", "s3", "af4", "s5", "r2", "b7", "r6", "f4", "m3", "vz1", "s4", "m5", "vz3", "p2",
    "vz2", "p6", "r3", "b2", "b6", "m4", "vz4", "r5", "p3", "vp", "b3", "r4", "p5", "vq", "b5", "p4", "fin",
)


def gelu_pair(preact):
    tangent = jnp.tanh(gelu_coef * (preact + cubic_coef * preact * preact * preact))
    gelu_value = 0.5 * preact * (1.0 + tangent)
    gelu_slope = 0.5 * (1.0 + tangent) + 0.5 * preact * (1.0 - tangent * tangent) * gelu_coef * (
        1.0 + 3.0 * cubic_coef * preact * preact
    )
    return (gelu_value, gelu_slope)


def kernel(
    tok_hbm, w_hbm, up_hbm,
    act_hbm, grad_hbm, last_tok_hbm, last_grad_hbm,
    xa, xb, wv, acc, own, give, got, part, share, grads, up1, up2, val2, val1,
    send_sem, recv_sem, load_sem, store_sem, act_sem, last_sem,
):
    row, col, depth = lax.axis_index("row"), lax.axis_index("col"), lax.axis_index("depth")
    y, zlo = lax.rem(row, 4), row // 4
    z = col * 2 + zlo
    x, core = depth // 2, lax.rem(depth, 2)

    def at(y_, z_, x_, core_):
        return (lax.rem(z_, 2) * 4 + y_, z_ // 2, x_ * 2 + core_)

    def y_to(k):
        return at(lax.rem(y + k, 4), z, x, core)

    def z_to(k):
        return at(y, lax.rem(z + k, 8), x, core)

    def x_to(k):
        return at(y, z, lax.rem(x + k, 4), core)

    def col_to(k):
        return (row, lax.rem(col + k, 4), depth)

    partner = at(y, z, x, 1 - core)
    numbers = {}
    sent = {}

    def copy(name, src, dst, device):
        n = numbers.setdefault(name, len(numbers))
        return pltpu.make_async_remote_copy(
            src_ref=src, dst_ref=dst, send_sem=send_sem.at[n], recv_sem=recv_sem.at[n],
            device_id=device, device_id_type=MESH,
        )

    def send(name, src, dst, device):
        c = copy(name, src, dst, device)
        c.start()
        sent[name] = c

    def arrive(name, dst):
        copy(name, dst, dst, partner).wait_recv()

    mine = pl.ds(pl.multiple_of(core * HALF, 128), HALF)
    theirs = pl.ds(pl.multiple_of((1 - core) * HALF, 128), HALF)
    halves = ((mine, pl.ds(0, HALF)), (theirs, pl.ds(HALF, HALF)))
    loads = [
        pltpu.make_async_copy(tok_hbm.at[:, pl.ds(0, KA)], xa.at[0, pl.ds(0, TOK)], load_sem.at[0]),
        pltpu.make_async_copy(tok_hbm.at[:, pl.ds(KA, KB)], xb.at[0, pl.ds(0, TOK)], load_sem.at[1]),
    ]
    for i, (there, here) in enumerate(halves):
        loads.append(pltpu.make_async_copy(w_hbm.at[:, there], wv.at[:, here], load_sem.at[2 + i]))

    def home_row(x_of, x_home):
        return lax.rem(y + x_of + col + 4 - x_home, 4)

    loads.append(pltpu.make_async_copy(up_hbm.at[:, home_row(x, x)], up1.at[x], load_sem.at[4]))
    for c in loads:
        c.start()

    barrier = pltpu.get_barrier_semaphore()
    others = (
        [y_to(1), y_to(3), z_to(1), z_to(7), partner]
        + [x_to(k) for k in (1, 2, 3)]
    )
    for other in others:
        pl.semaphore_signal(barrier, inc=1, device_id=other, device_id_type=MESH)
    pl.semaphore_wait(barrier, len(others))

    LOW, HIGH = pl.ds(0, 32), pl.ds(32, 32)

    def rows(dy, lo=0, n=TOK):
        return pl.ds(dy * TOK + lo, n)

    def a_along_z(k):
        down, up = (k - 1) % 8, (1 - k) % 8
        if k < 4:
            send(("az-", k), xa.at[down, rows(0)], xa.at[k, rows(0)], z_to(7))
            send(("az+", k), xa.at[up, rows(0)], xa.at[8 - k, rows(0)], z_to(1))
        else:
            send(("az-", 4), xa.at[3, LOW], xa.at[4, LOW], z_to(7))
            send(("az+", 4), xa.at[5, HIGH], xa.at[4, HIGH], z_to(1))

    def a_from_z(k):
        if k < 4:
            arrive(("az-", k), xa.at[k, rows(0)])
            arrive(("az+", k), xa.at[8 - k, rows(0)])
        else:
            arrive(("az-", 4), xa.at[4, LOW])
            arrive(("az+", 4), xa.at[4, HIGH])

    def a_along_y(dz):
        send(("ay-", dz), xa.at[dz, rows(0)], xa.at[dz, rows(1)], y_to(3))
        send(("ay+", dz), xa.at[dz, rows(0)], xa.at[dz, rows(3)], y_to(1))

    def a_from_y(dz):
        arrive(("ay-", dz), xa.at[dz, rows(1)])
        arrive(("ay+", dz), xa.at[dz, rows(3)])

    def a_far_y(dz):
        send(("af-", dz), xa.at[dz, rows(1, 0, 32)], xa.at[dz, rows(2, 0, 32)], y_to(3))
        send(("af+", dz), xa.at[dz, rows(3, 32, 32)], xa.at[dz, rows(2, 32, 32)], y_to(1))

    def a_from_far(dz):
        arrive(("af-", dz), xa.at[dz, rows(2, 0, 32)])
        arrive(("af+", dz), xa.at[dz, rows(2, 32, 32)])

    def b_along_y():
        send("by-", xb.at[0, rows(0)], xb.at[0, rows(1)], y_to(3))
        send("by+", xb.at[0, rows(0)], xb.at[0, rows(3)], y_to(1))

    def b_from_y():
        arrive("by-", xb.at[0, rows(1)])
        arrive("by+", xb.at[0, rows(3)])

    def b_far_y():
        send("bf-", xb.at[0, rows(1, 0, 32)], xb.at[0, rows(2, 0, 32)], y_to(3))
        send("bf+", xb.at[0, rows(3, 32, 32)], xb.at[0, rows(2, 32, 32)], y_to(1))

    def b_from_far():
        arrive("bf-", xb.at[0, rows(2, 0, 32)])
        arrive("bf+", xb.at[0, rows(2, 32, 32)])

    HALVES = (pl.ds(0, 128), pl.ds(128, 128))

    def b_along_z(k, h):
        down, up, part_rows = (k - 1) % 8, (1 - k) % 8, HALVES[h]
        send(("bz-", k, h), xb.at[down, part_rows], xb.at[k, part_rows], z_to(7))
        send(("bz+", k, h), xb.at[up, part_rows], xb.at[8 - k, part_rows], z_to(1))

    def b_from_z(k, h):
        arrive(("bz-", k, h), xb.at[k, HALVES[h]])
        arrive(("bz+", k, h), xb.at[8 - k, HALVES[h]])

    def b_far_z():
        send("bq-", xb.at[3, HALVES[0]], xb.at[4, HALVES[0]], z_to(7))
        send("bq+", xb.at[5, HALVES[1]], xb.at[4, HALVES[1]], z_to(1))

    def b_from_far_z():
        arrive("bq-", xb.at[4, HALVES[0]])
        arrive("bq+", xb.at[4, HALVES[1]])

    def up_along_x():
        for k in (1, 2, 3):
            there = lax.rem(x + k, 4)
            send(("ux", k), up_hbm.at[:, home_row(there, x)], up1.at[x], x_to(k))

    def up_from_x():
        loads[4].wait()
        for k in (1, 2, 3):
            arrive(("ux", k), up1.at[lax.rem(x + 4 - k, 4)])

    stay = pltpu.make_async_copy(up1.at[col], up2.at[0], load_sem.at[5])

    def up_along_z(ks):
        for k in ks:
            send(("uz", k), up1.at[lax.rem(col + k, 4)], up2.at[4 - k], col_to(k))

    def up_from_z(ks):
        for k in ks:
            arrive(("uz", k), up2.at[4 - k])

    def act_along_z(delta):
        if delta == 0:
            act_stay.start()
        else:
            send(("vz", delta), val2.at[delta], val1.at[col], col_to(delta))

    def act_half_along_z(odd, name):
        send((name, 2), val2.at[2, odd], val1.at[col, odd], col_to(2))

    def act_from_z(delta):
        arrive(("vz", delta), val1.at[lax.rem(col + 4 - delta, 4)])

    def act_half_from_z(odd, name):
        arrive((name, 2), val1.at[lax.rem(col + 2, 4), odd])

    def act_along_x(odd, name):
        for k in (1, 2, 3):
            there = lax.rem(x + k, 4)
            send((name, k), val1.at[there, odd], act_hbm.at[odd, home_row(x, there)], x_to(k))

    act_stay = pltpu.make_async_copy(val2.at[0], val1.at[col], act_sem.at[0])
    act_here = pltpu.make_async_copy(val1.at[x], act_hbm.at[:, home_row(x, x)], act_sem.at[1])

    def act_late():
        act_along_x(zlo, "vq")
        act_here.start()

    def act_done():
        act_here.wait()
        for odd, name in ((1 - zlo, "vp"), (zlo, "vq")):
            for k in (1, 2, 3):
                arrive((name, k), act_hbm.at[odd, home_row(lax.rem(x + 4 - k, 4), x)])

    def delta_of(dz):
        return lax.rem((zlo + dz) // 2, 4)

    def chunk_rows(dz, x_of):
        dy = lax.rem(x_of + delta_of(dz), 4)
        return pl.ds(pl.multiple_of(dy * TOK, TOK), TOK)

    def forward(dz):
        for n in range(3):
            columns = pl.ds(n * 256, 256)
            value = jnp.dot(xa[dz], wv[pl.ds(0, KA), columns], preferred_element_type=jnp.float32)
            value = value + jnp.dot(xb[dz], wv[pl.ds(KA, KB), columns], preferred_element_type=jnp.float32)
            if n == 0:
                own[dz, :, pl.ds(0, 256)] = value
            elif n == 1:
                own[dz, :, pl.ds(256, 128)] = value[:, :128]
                give[dz, :, pl.ds(0, 128)] = value[:, 128:].astype(jnp.bfloat16)
            else:
                give[dz, :, pl.ds(128, 256)] = value.astype(jnp.bfloat16)
        send(("pair", dz), give.at[dz], got.at[dz], partner)

    def scatter(dz):
        total = own[dz] + got[dz].astype(jnp.float32)
        own[dz] = total
        part[dz] = total.astype(jnp.bfloat16)
        for k in (1, 2, 3):
            chunk = chunk_rows(dz, lax.rem(x + k, 4))
            send(("sum", dz, k), part.at[dz, chunk], share.at[dz, k - 1], x_to(k))

    def middle(dz):
        chunk = chunk_rows(dz, x)
        summed = own[dz, chunk, :]
        for k in range(3):
            summed = summed + share[dz, k].astype(jnp.float32)
        gelu_value, gelu_slope = gelu_pair(summed * fan_scale)
        delta, odd = delta_of(dz), lax.rem(zlo + dz, 2)
        val2[delta, odd] = gelu_value.astype(jnp.bfloat16)
        grads[dz, 0, chunk, :] = (up2[delta, odd].astype(jnp.float32) * gelu_slope).astype(jnp.bfloat16)
        for k in (1, 3):
            send(("grad", dz, k), grads.at[dz, 0, chunk], grads.at[dz, 0, chunk], x_to(k))

    def half_chunk(dz, x_of, lo):
        dy = lax.rem(x_of + delta_of(dz), 4)
        return pl.ds(pl.multiple_of(dy * TOK + lo, 32), 32)

    def relay(dz):
        low, high = half_chunk(dz, lax.rem(x + 3, 4), 0), half_chunk(dz, lax.rem(x + 1, 4), 32)
        send(("far", dz, 1), grads.at[dz, 0, low], grads.at[dz, 0, low], x_to(1))
        send(("far", dz, 3), grads.at[dz, 0, high], grads.at[dz, 0, high], x_to(3))

    def far_from(dz):
        far = lax.rem(x + 2, 4)
        arrive(("far", dz, 1), grads.at[dz, 0, half_chunk(dz, far, 0)])
        arrive(("far", dz, 3), grads.at[dz, 0, half_chunk(dz, far, 32)])

    def pass_on(dz):
        send(("both", dz), grads.at[dz, 0], grads.at[dz, 1], partner)

    def gradient_tile(dz, tile):
        both = jnp.concatenate([grads[dz, 0], grads[dz, 1]], axis=1)
        if isinstance(tile, tuple):
            source, columns = tile
        return lax.dot_general(
            source[dz, :, columns], both, (((0,), (0,)), ((), ())), preferred_element_type=jnp.float32
        )

    TILE = 256
    begun = []

    def backward(dz):
        first = not begun
        begun.append(dz)
        last = len(begun) == 7

        for source, base, count in ((xa, 0, KA // TILE), (xb, KA, KB // TILE)):
            @pl.loop(0, count)
            def _(t):
                columns = pl.ds(pl.multiple_of(t * TILE, TILE), TILE)
                out = pl.ds(pl.multiple_of(base + t * TILE, TILE), TILE)
                value = gradient_tile(dz, (source, columns))
                acc[out, :] = value if first else acc[out, :] + value
                if last:
                    for c in stores(base // TILE + t):
                        c.start()

    def stores(tile):
        out = pl.ds(pl.multiple_of(tile * TILE, TILE), TILE)
        result = []
        for i, (there, here) in enumerate(halves):
            result.append(pltpu.make_async_copy(acc.at[out, here], grad_hbm.at[out, there], store_sem.at[tile, i]))
        return result

    last_tok = [
        pltpu.make_async_copy(xa.at[4], last_tok_hbm.at[:, pl.ds(0, KA)], last_sem.at[0]),
        pltpu.make_async_copy(xb.at[4], last_tok_hbm.at[:, pl.ds(KA, KB)], last_sem.at[1]),
    ]
    last_grad = [
        pltpu.make_async_copy(grads.at[4, 0], last_grad_hbm.at[:, mine], last_sem.at[2]),
        pltpu.make_async_copy(grads.at[4, 1], last_grad_hbm.at[:, theirs], last_sem.at[3]),
    ]

    def forward_last():
        forward(4)
        for c in last_tok:
            c.start()

    def finish():
        for c in last_grad:
            c.start()

    def sums_from(dz):
        for k in (1, 2, 3):
            arrive(("sum", dz, k), share.at[dz, k - 1])

    def grads_from(dz):
        for k in (1, 3):
            arrive(("grad", dz, k), grads.at[dz, 0, chunk_rows(dz, lax.rem(x + 4 - k, 4))])

    def wait_all(copies):
        for c in copies:
            c.wait()

    received = {
        "tok_a": loads[0].wait, "tok_b": loads[1].wait, "by": b_from_y, "bf": b_from_far, "bz4": b_from_far_z,
        "ux": up_from_x, "uz0": stay.wait, "uz1": lambda: up_from_z((1, 3)), "uz2": lambda: up_from_z((2,)),
        "w": lambda: wait_all(loads[2:4]),
    }
    for k in (1, 2, 3, 4):
        received[f"az{k}"] = functools.partial(a_from_z, k)
        for h in (0, 1):
            received[f"bz{k}{h}"] = functools.partial(b_from_z, k, h)
    for dz in range(8):
        received[f"ay{dz}"] = functools.partial(a_from_y, dz)
        received[f"af{dz}"] = functools.partial(a_from_far, dz)
        received[f"pair{dz}"] = functools.partial(lambda d: arrive(("pair", d), got.at[d]), dz)
        received[f"sum{dz}"] = functools.partial(sums_from, dz)
        received[f"near{dz}"] = functools.partial(grads_from, dz)
        received[f"grad{dz}"] = functools.partial(far_from, dz)
        received[f"both{dz}"] = functools.partial(lambda d: arrive(("both", d), grads.at[d, 1]), dz)
    for delta in (1, 2, 3):
        received[f"vz{delta}"] = functools.partial(act_from_z, delta)

    def begin():
        need("tok_a")
        a_along_z(1)
        need("tok_b")
        b_along_y()
        a_along_y(0)
        up_along_x()

    events = {
        "start": ((), begin),
        "bfar": (("by",), b_far_y),
        "bz4": (("bz30", "bz31"), b_far_z),
        "u0": (("ux",), stay.start),
        "uz1": (("ux", "az2"), lambda: up_along_z((1, 3))),
        "uz2": (("ux", "az4"), lambda: up_along_z((2,))),
        "vp": (("vz0", "vz1", "vz2", "vz3"), lambda: act_along_x(1 - zlo, "vp")),
        "vq": (("vz4",), act_late),
        "fin": (("both4",), finish),
    }
    for k in (2, 3, 4):
        events[f"az{k}"] = ((f"az{k - 1}",), functools.partial(a_along_z, k))
    for h in (0, 1):
        events[f"bz1{h}"] = (("by", "bf") if h else ("by",), functools.partial(b_along_z, 1, h))
        for k in (2, 3):
            events[f"bz{k}{h}"] = ((f"bz{k - 1}{h}",), functools.partial(b_along_z, k, h))
    for dz in range(8):
        k = min(dz, 8 - dz)
        lower = {0: ("by", "bf"), 4: ("bz4",)}.get(k, (f"bz{k}0", f"bz{k}1"))
        upper = {0: ("uz0",), 1: ("uz0", "uz1"), 2: ("uz1",), 3: ("uz1", "uz2"), 4: ("uz2",)}[k]
        if dz:
            events[f"ay{dz}"] = ((f"az{k}",), functools.partial(a_along_y, dz))
        events[f"af{dz}"] = ((f"ay{dz}",), functools.partial(a_far_y, dz))
        events[f"f{dz}"] = (("w", f"af{dz}") + lower, functools.partial(forward, dz))
        events[f"s{dz}"] = ((f"pair{dz}",), functools.partial(scatter, dz))
        events[f"m{dz}"] = ((f"sum{dz}",) + upper, functools.partial(middle, dz))
        events[f"r{dz}"] = ((f"near{dz}",), functools.partial(relay, dz))
        events[f"p{dz}"] = ((f"grad{dz}",), functools.partial(pass_on, dz))
        events[f"b{dz}"] = ((f"both{dz}",), functools.partial(backward, dz))
    events["f4"] = (events["f4"][0], forward_last)
    for delta in range(4):
        events[f"vz{delta}"] = ((), functools.partial(act_along_z, delta))
    events["vz2"] = ((), functools.partial(act_half_along_z, 1 - zlo, "va"))
    events["vz4"] = ((), functools.partial(act_half_along_z, zlo, "vb"))
    received["vz0"] = act_stay.wait
    received["vz2"] = functools.partial(act_half_from_z, 1 - zlo, "va")
    received["vz4"] = functools.partial(act_half_from_z, zlo, "vb")

    had = set()

    def need(name):
        if name not in had:
            had.add(name)
            received[name]()

    for name in ORDER:
        needs, do = events[name]
        for other in needs:
            need(other)
        do()
    act_done()
    for tile in range(FEAT // TILE):
        for c in stores(tile):
            c.wait()
    for c in last_tok + last_grad:
        c.wait()
    for c in sent.values():
        c.wait_send()
    assert len(numbers) <= NSEM, len(numbers)


def update(act_in, tok_ref, grad_ref, sum_ref, w_ref, m_ref, act_out, nw_ref, nm_ref, act_sem):
    step = pl.program_id(0)
    act = pltpu.make_async_copy(act_in, act_out, act_sem)

    @pl.when(step == 0)
    def _():
        act.start()

    grad_sum = sum_ref[...] + lax.dot_general(
        tok_ref[...], grad_ref[...], (((0,), (0,)), ((), ())), preferred_element_type=jnp.float32
    )
    moment_f = m_ref[...].astype(jnp.float32)
    weight_f = w_ref[...].astype(jnp.float32)
    blended = beta_one * moment_f + ((1.0 - beta_one) * fan_scale) * grad_sum
    sign = blended * lax.rsqrt(blended * blended + smooth_tau * smooth_tau)
    nw_ref[...] = ((1.0 - lion_rate * decay_rate) * weight_f - lion_rate * sign).astype(jnp.bfloat16)
    nm_ref[...] = (beta_two * moment_f + ((1.0 - beta_two) * fan_scale) * grad_sum).astype(jnp.bfloat16)

    @pl.when(step == pl.num_programs(0) - 1)
    def _():
        act.wait()


def shards(tokens, weight, moment, upstream):
    bf16, f32 = jnp.bfloat16, jnp.float32
    any_space = pl.BlockSpec(memory_space=pl.ANY)
    act_shape = jax.ShapeDtypeStruct((2, 4, TOK, HALF), bf16)
    block_shape = jax.ShapeDtypeStruct((FEAT, HID), bf16)
    act, grad_sum, last_tok, last_grad = pl.pallas_call(
        kernel,
        out_shape=(
            act_shape,
            jax.ShapeDtypeStruct((FEAT, HID), f32),
            jax.ShapeDtypeStruct((PIECE, FEAT), bf16),
            jax.ShapeDtypeStruct((PIECE, HID), bf16),
        ),
        in_specs=[any_space] * 3,
        out_specs=(any_space,) * 4,
        scratch_shapes=[
            pltpu.VMEM((8, PIECE, KA), bf16),
            pltpu.VMEM((8, PIECE, KB), bf16),
            pltpu.VMEM((FEAT, HID), bf16),
            pltpu.VMEM((FEAT, HID), f32),
            pltpu.VMEM((8, PIECE, HALF), f32),
            pltpu.VMEM((8, PIECE, HALF), bf16),
            pltpu.VMEM((8, PIECE, HALF), bf16),
            pltpu.VMEM((8, PIECE, HALF), bf16),
            pltpu.VMEM((8, 3, TOK, HALF), bf16),
            pltpu.VMEM((8, 2, PIECE, HALF), bf16),
            pltpu.VMEM((4, 2, TOK, HALF), bf16),
            pltpu.VMEM((4, 2, TOK, HALF), bf16),
            pltpu.VMEM((4, 2, TOK, HALF), bf16),
            pltpu.VMEM((4, 2, TOK, HALF), bf16),
            pltpu.SemaphoreType.DMA((NSEM,)),
            pltpu.SemaphoreType.DMA((NSEM,)),
            pltpu.SemaphoreType.DMA((6,)),
            pltpu.SemaphoreType.DMA((FEAT // 256, 2)),
            pltpu.SemaphoreType.DMA((2,)),
            pltpu.SemaphoreType.DMA((4,)),
        ],
        compiler_params=pltpu.CompilerParams(
            collective_id=0, has_side_effects=True, vmem_limit_bytes=44 * 1024 * 1024
        ),
        cost_estimate=pl.CostEstimate(
            flops=4 * 2048 * FEAT * HID, bytes_accessed=12 * 1024 * 1024, transcendentals=2 * FEAT * HID
        ),
    )(tokens, weight, upstream.reshape(2, 4, TOK, HALF))
    tile = pl.BlockSpec((UPDATE, HID), lambda t: (t, 0))
    act, new_weight, new_moment = pl.pallas_call(
        update,
        out_shape=(act_shape, block_shape, block_shape),
        grid=(FEAT // UPDATE,),
        in_specs=[
            any_space,
            pl.BlockSpec((PIECE, UPDATE), lambda t: (0, t)),
            pl.BlockSpec((PIECE, HID), lambda t: (0, 0)),
            tile,
            tile,
            tile,
        ],
        out_specs=(any_space, tile, tile),
        scratch_shapes=[pltpu.SemaphoreType.DMA],
        compiler_params=pltpu.CompilerParams(vmem_limit_bytes=16 * 1024 * 1024),
        cost_estimate=pl.CostEstimate(
            flops=2 * PIECE * FEAT * HID, bytes_accessed=16 * FEAT * HID, transcendentals=FEAT * HID
        ),
    )(act, last_tok, last_grad, grad_sum, weight, moment)
    return (act.reshape(upstream.shape), new_weight, new_moment)


def solution(mesh):
    placed = (
        P(("row", "col"), "depth"),
        P("depth", ("row", "col")),
        P("depth", ("row", "col")),
        P(None, "col", ("row", "depth")),
    )
    return jax.shard_map(
        shards,
        mesh=mesh,
        in_specs=placed,
        out_specs=(
            P(None, "col", ("row", "depth")),
            P("depth", ("row", "col")),
            P("depth", ("row", "col")),
        ),
        check_vma=False,
    )
```

```python
import functools

import jax
import jax.numpy as jnp
from jax import lax
from jax.experimental import pallas as pl
from jax.experimental.pallas import tpu as pltpu
from jax.sharding import PartitionSpec as P

D = 12288
TOK = 64
KA = 1024
KB = 512
FEAT = 1536
HID = 768
HALF = 384
PIECE = 256
NSEM = 176
UPDATE = 256

gelu_coef = 0.7978845608028654
cubic_coef = 0.044715
lion_rate = 0.5
decay_rate = 0.1
beta_one = 0.9
beta_two = 0.99
smooth_tau = 0.1
fan_scale = D ** (-0.5)

MESH = pl.DeviceIdType.MESH

ORDER = (
    "start", "bfar", "bz10", "ay1", "az2", "af0", "ay7", "u0", "bz11", "bz20", "af1", "az3", "uz1", "ay2", "f0",
    "bz21", "af7", "ay6", "s0", "f1", "bz30", "af2", "s1", "m0", "az4", "ay3", "f7", "af6", "ay5", "s7", "r0", "m1",
    "bz31", "af3", "f2", "f6", "m7", "p0", "vz0", "r1", "s2", "uz2", "af5", "ay4", "s6", "b0", "r7", "p1", "bz4",
    "f3", "f5", "b1", "m2", "s3", "af4", "s5", "m6", "p7", "r2", "b7", "f4", "m3", "vz1", "s4", "m5", "vz3", "vz2",
    "r6", "p2", "r3", "b2", "m4", "vz4", "r5", "p6", "p3", "vp", "b6", "r4", "b3", "p5", "vq", "p4", "b5", "fin",
)


def gelu_pair(preact):
    tangent = jnp.tanh(gelu_coef * (preact + cubic_coef * preact * preact * preact))
    gelu_value = 0.5 * preact * (1.0 + tangent)
    gelu_slope = 0.5 * (1.0 + tangent) + 0.5 * preact * (1.0 - tangent * tangent) * gelu_coef * (
        1.0 + 3.0 * cubic_coef * preact * preact
    )
    return (gelu_value, gelu_slope)


def kernel(
    tok_hbm, w_hbm, up_hbm,
    act_hbm, grad_hbm, last_tok_hbm, last_grad_hbm,
    xa, xb, wv, acc, own, give, got, part, share, grads, up1, up2, val2, val1,
    send_sem, recv_sem, load_sem, store_sem, act_sem, last_sem,
):
    row, col, depth = lax.axis_index("row"), lax.axis_index("col"), lax.axis_index("depth")
    y, zlo = lax.rem(row, 4), row // 4
    z = col * 2 + zlo
    x, core = depth // 2, lax.rem(depth, 2)

    def at(y_, z_, x_, core_):
        return (lax.rem(z_, 2) * 4 + y_, z_ // 2, x_ * 2 + core_)

    def y_to(k):
        return at(lax.rem(y + k, 4), z, x, core)

    def z_to(k):
        return at(y, lax.rem(z + k, 8), x, core)

    def x_to(k):
        return at(y, z, lax.rem(x + k, 4), core)

    def col_to(k):
        return (row, lax.rem(col + k, 4), depth)

    partner = at(y, z, x, 1 - core)
    numbers = {}
    sent = {}

    def copy(name, src, dst, device):
        n = numbers.setdefault(name, len(numbers))
        return pltpu.make_async_remote_copy(
            src_ref=src, dst_ref=dst, send_sem=send_sem.at[n], recv_sem=recv_sem.at[n],
            device_id=device, device_id_type=MESH,
        )

    def send(name, src, dst, device):
        c = copy(name, src, dst, device)
        c.start()
        sent[name] = c

    def arrive(name, dst):
        copy(name, dst, dst, partner).wait_recv()

    mine = pl.ds(pl.multiple_of(core * HALF, 128), HALF)
    theirs = pl.ds(pl.multiple_of((1 - core) * HALF, 128), HALF)
    halves = ((mine, pl.ds(0, HALF)), (theirs, pl.ds(HALF, HALF)))
    loads = [
        pltpu.make_async_copy(tok_hbm.at[:, pl.ds(0, KA)], xa.at[0, pl.ds(0, TOK)], load_sem.at[0]),
        pltpu.make_async_copy(tok_hbm.at[:, pl.ds(KA, KB)], xb.at[0, pl.ds(0, TOK)], load_sem.at[1]),
    ]
    for i, (there, here) in enumerate(halves):
        loads.append(pltpu.make_async_copy(w_hbm.at[:, there], wv.at[:, here], load_sem.at[2 + i]))

    def home_row(x_of, x_home):
        return lax.rem(y + x_of + col + 4 - x_home, 4)

    loads.append(pltpu.make_async_copy(up_hbm.at[:, home_row(x, x)], up1.at[x], load_sem.at[4]))
    for c in loads:
        c.start()

    barrier = pltpu.get_barrier_semaphore()
    others = (
        [y_to(1), y_to(3), z_to(1), z_to(7), partner]
        + [x_to(k) for k in (1, 2, 3)]
    )
    for other in others:
        pl.semaphore_signal(barrier, inc=1, device_id=other, device_id_type=MESH)
    pl.semaphore_wait(barrier, len(others))

    LOW, HIGH = pl.ds(0, 32), pl.ds(32, 32)

    def rows(dy, lo=0, n=TOK):
        return pl.ds(dy * TOK + lo, n)

    def a_along_z(k):
        down, up = (k - 1) % 8, (1 - k) % 8
        if k < 4:
            send(("az-", k), xa.at[down, rows(0)], xa.at[k, rows(0)], z_to(7))
            send(("az+", k), xa.at[up, rows(0)], xa.at[8 - k, rows(0)], z_to(1))
        else:
            send(("az-", 4), xa.at[3, LOW], xa.at[4, LOW], z_to(7))
            send(("az+", 4), xa.at[5, HIGH], xa.at[4, HIGH], z_to(1))

    def a_from_z(k):
        if k < 4:
            arrive(("az-", k), xa.at[k, rows(0)])
            arrive(("az+", k), xa.at[8 - k, rows(0)])
        else:
            arrive(("az-", 4), xa.at[4, LOW])
            arrive(("az+", 4), xa.at[4, HIGH])

    def a_along_y(dz):
        send(("ay-", dz), xa.at[dz, rows(0)], xa.at[dz, rows(1)], y_to(3))
        send(("ay+", dz), xa.at[dz, rows(0)], xa.at[dz, rows(3)], y_to(1))

    def a_from_y(dz):
        arrive(("ay-", dz), xa.at[dz, rows(1)])
        arrive(("ay+", dz), xa.at[dz, rows(3)])

    def a_far_y(dz):
        send(("af-", dz), xa.at[dz, rows(1, 0, 32)], xa.at[dz, rows(2, 0, 32)], y_to(3))
        send(("af+", dz), xa.at[dz, rows(3, 32, 32)], xa.at[dz, rows(2, 32, 32)], y_to(1))

    def a_from_far(dz):
        arrive(("af-", dz), xa.at[dz, rows(2, 0, 32)])
        arrive(("af+", dz), xa.at[dz, rows(2, 32, 32)])

    def b_along_y():
        send("by-", xb.at[0, rows(0)], xb.at[0, rows(1)], y_to(3))
        send("by+", xb.at[0, rows(0)], xb.at[0, rows(3)], y_to(1))

    def b_from_y():
        arrive("by-", xb.at[0, rows(1)])
        arrive("by+", xb.at[0, rows(3)])

    def b_far_y():
        send("bf-", xb.at[0, rows(1, 0, 32)], xb.at[0, rows(2, 0, 32)], y_to(3))
        send("bf+", xb.at[0, rows(3, 32, 32)], xb.at[0, rows(2, 32, 32)], y_to(1))

    def b_from_far():
        arrive("bf-", xb.at[0, rows(2, 0, 32)])
        arrive("bf+", xb.at[0, rows(2, 32, 32)])

    HALVES = (pl.ds(0, 128), pl.ds(128, 128))

    def b_along_z(k, h):
        down, up, part_rows = (k - 1) % 8, (1 - k) % 8, HALVES[h]
        send(("bz-", k, h), xb.at[down, part_rows], xb.at[k, part_rows], z_to(7))
        send(("bz+", k, h), xb.at[up, part_rows], xb.at[8 - k, part_rows], z_to(1))

    def b_from_z(k, h):
        arrive(("bz-", k, h), xb.at[k, HALVES[h]])
        arrive(("bz+", k, h), xb.at[8 - k, HALVES[h]])

    def b_far_z():
        send("bq-", xb.at[3, HALVES[0]], xb.at[4, HALVES[0]], z_to(7))
        send("bq+", xb.at[5, HALVES[1]], xb.at[4, HALVES[1]], z_to(1))

    def b_from_far_z():
        arrive("bq-", xb.at[4, HALVES[0]])
        arrive("bq+", xb.at[4, HALVES[1]])

    def up_along_x():
        for k in (1, 2, 3):
            there = lax.rem(x + k, 4)
            send(("ux", k), up_hbm.at[:, home_row(there, x)], up1.at[x], x_to(k))

    def up_from_x():
        loads[4].wait()
        for k in (1, 2, 3):
            arrive(("ux", k), up1.at[lax.rem(x + 4 - k, 4)])

    stay = pltpu.make_async_copy(up1.at[col], up2.at[0], load_sem.at[5])

    def up_along_z(ks):
        for k in ks:
            send(("uz", k), up1.at[lax.rem(col + k, 4)], up2.at[4 - k], col_to(k))

    def up_from_z(ks):
        for k in ks:
            arrive(("uz", k), up2.at[4 - k])

    def act_along_z(delta):
        if delta == 0:
            act_stay.start()
        else:
            send(("vz", delta), val2.at[delta], val1.at[col], col_to(delta))

    def act_half_along_z(odd, name):
        send((name, 2), val2.at[2, odd], val1.at[col, odd], col_to(2))

    def act_from_z(delta):
        arrive(("vz", delta), val1.at[lax.rem(col + 4 - delta, 4)])

    def act_half_from_z(odd, name):
        arrive((name, 2), val1.at[lax.rem(col + 2, 4), odd])

    def act_along_x(odd, name):
        for k in (1, 2, 3):
            there = lax.rem(x + k, 4)
            send((name, k), val1.at[there, odd], act_hbm.at[odd, home_row(x, there)], x_to(k))

    act_stay = pltpu.make_async_copy(val2.at[0], val1.at[col], act_sem.at[0])
    act_here = pltpu.make_async_copy(val1.at[x], act_hbm.at[:, home_row(x, x)], act_sem.at[1])

    def act_late():
        act_along_x(zlo, "vq")
        act_here.start()

    def act_done():
        act_here.wait()
        for odd, name in ((1 - zlo, "vp"), (zlo, "vq")):
            for k in (1, 2, 3):
                arrive((name, k), act_hbm.at[odd, home_row(lax.rem(x + 4 - k, 4), x)])

    def delta_of(dz):
        return lax.rem((zlo + dz) // 2, 4)

    def chunk_rows(dz, x_of):
        dy = lax.rem(x_of + delta_of(dz), 4)
        return pl.ds(pl.multiple_of(dy * TOK, TOK), TOK)

    def forward(dz):
        for n in range(3):
            columns = pl.ds(n * 256, 256)
            value = jnp.dot(xa[dz], wv[pl.ds(0, KA), columns], preferred_element_type=jnp.float32)
            value = value + jnp.dot(xb[dz], wv[pl.ds(KA, KB), columns], preferred_element_type=jnp.float32)
            if n == 0:
                own[dz, :, pl.ds(0, 256)] = value
            elif n == 1:
                own[dz, :, pl.ds(256, 128)] = value[:, :128]
                give[dz, :, pl.ds(0, 128)] = value[:, 128:].astype(jnp.bfloat16)
            else:
                give[dz, :, pl.ds(128, 256)] = value.astype(jnp.bfloat16)
        send(("pair", dz), give.at[dz], got.at[dz], partner)

    def scatter(dz):
        total = own[dz] + got[dz].astype(jnp.float32)
        own[dz] = total
        part[dz] = total.astype(jnp.bfloat16)
        for k in (1, 2, 3):
            chunk = chunk_rows(dz, lax.rem(x + k, 4))
            send(("sum", dz, k), part.at[dz, chunk], share.at[dz, k - 1], x_to(k))

    def middle(dz):
        chunk = chunk_rows(dz, x)
        summed = own[dz, chunk, :]
        for k in range(3):
            summed = summed + share[dz, k].astype(jnp.float32)
        gelu_value, gelu_slope = gelu_pair(summed * fan_scale)
        delta, odd = delta_of(dz), lax.rem(zlo + dz, 2)
        val2[delta, odd] = gelu_value.astype(jnp.bfloat16)
        grads[dz, 0, chunk, :] = (up2[delta, odd].astype(jnp.float32) * gelu_slope).astype(jnp.bfloat16)
        for k in (1, 3):
            send(("grad", dz, k), grads.at[dz, 0, chunk], grads.at[dz, 0, chunk], x_to(k))

    def half_chunk(dz, x_of, lo):
        dy = lax.rem(x_of + delta_of(dz), 4)
        return pl.ds(pl.multiple_of(dy * TOK + lo, 32), 32)

    def relay(dz):
        low, high = half_chunk(dz, lax.rem(x + 3, 4), 0), half_chunk(dz, lax.rem(x + 1, 4), 32)
        send(("far", dz, 1), grads.at[dz, 0, low], grads.at[dz, 0, low], x_to(1))
        send(("far", dz, 3), grads.at[dz, 0, high], grads.at[dz, 0, high], x_to(3))

    def far_from(dz):
        far = lax.rem(x + 2, 4)
        arrive(("far", dz, 1), grads.at[dz, 0, half_chunk(dz, far, 0)])
        arrive(("far", dz, 3), grads.at[dz, 0, half_chunk(dz, far, 32)])

    def pass_on(dz):
        send(("both", dz), grads.at[dz, 0], grads.at[dz, 1], partner)

    def gradient_tile(dz, tile):
        both = jnp.concatenate([grads[dz, 0], grads[dz, 1]], axis=1)
        if isinstance(tile, tuple):
            source, columns = tile
        return lax.dot_general(
            source[dz, :, columns], both, (((0,), (0,)), ((), ())), preferred_element_type=jnp.float32
        )

    TILE = 256
    begun = []

    def backward(dz):
        first = not begun
        begun.append(dz)
        last = len(begun) == 7

        for source, base, count in ((xa, 0, KA // TILE), (xb, KA, KB // TILE)):
            @pl.loop(0, count)
            def _(t):
                columns = pl.ds(pl.multiple_of(t * TILE, TILE), TILE)
                out = pl.ds(pl.multiple_of(base + t * TILE, TILE), TILE)
                value = gradient_tile(dz, (source, columns))
                acc[out, :] = value if first else acc[out, :] + value
                if last:
                    for c in stores(base // TILE + t):
                        c.start()

    def stores(tile):
        out = pl.ds(pl.multiple_of(tile * TILE, TILE), TILE)
        result = []
        for i, (there, here) in enumerate(halves):
            result.append(pltpu.make_async_copy(acc.at[out, here], grad_hbm.at[out, there], store_sem.at[tile, i]))
        return result

    last_tok = [
        pltpu.make_async_copy(xa.at[4], last_tok_hbm.at[:, pl.ds(0, KA)], last_sem.at[0]),
        pltpu.make_async_copy(xb.at[4], last_tok_hbm.at[:, pl.ds(KA, KB)], last_sem.at[1]),
    ]
    last_grad = [
        pltpu.make_async_copy(grads.at[4, 0], last_grad_hbm.at[:, mine], last_sem.at[2]),
        pltpu.make_async_copy(grads.at[4, 1], last_grad_hbm.at[:, theirs], last_sem.at[3]),
    ]

    def forward_last():
        forward(4)
        for c in last_tok:
            c.start()

    def finish():
        for c in last_grad:
            c.start()

    def sums_from(dz):
        for k in (1, 2, 3):
            arrive(("sum", dz, k), share.at[dz, k - 1])

    def grads_from(dz):
        for k in (1, 3):
            arrive(("grad", dz, k), grads.at[dz, 0, chunk_rows(dz, lax.rem(x + 4 - k, 4))])

    def wait_all(copies):
        for c in copies:
            c.wait()

    received = {
        "tok_a": loads[0].wait, "tok_b": loads[1].wait, "by": b_from_y, "bf": b_from_far, "bz4": b_from_far_z,
        "ux": up_from_x, "uz0": stay.wait, "uz1": lambda: up_from_z((1, 3)), "uz2": lambda: up_from_z((2,)),
        "w": lambda: wait_all(loads[2:4]),
    }
    for k in (1, 2, 3, 4):
        received[f"az{k}"] = functools.partial(a_from_z, k)
        for h in (0, 1):
            received[f"bz{k}{h}"] = functools.partial(b_from_z, k, h)
    for dz in range(8):
        received[f"ay{dz}"] = functools.partial(a_from_y, dz)
        received[f"af{dz}"] = functools.partial(a_from_far, dz)
        received[f"pair{dz}"] = functools.partial(lambda d: arrive(("pair", d), got.at[d]), dz)
        received[f"sum{dz}"] = functools.partial(sums_from, dz)
        received[f"near{dz}"] = functools.partial(grads_from, dz)
        received[f"grad{dz}"] = functools.partial(far_from, dz)
        received[f"both{dz}"] = functools.partial(lambda d: arrive(("both", d), grads.at[d, 1]), dz)
    for delta in (1, 2, 3):
        received[f"vz{delta}"] = functools.partial(act_from_z, delta)

    def begin():
        need("tok_a")
        a_along_z(1)
        need("tok_b")
        b_along_y()
        a_along_y(0)
        up_along_x()

    events = {
        "start": ((), begin),
        "bfar": (("by",), b_far_y),
        "bz4": (("bz30", "bz31"), b_far_z),
        "u0": (("ux",), stay.start),
        "uz1": (("ux", "az2"), lambda: up_along_z((1, 3))),
        "uz2": (("ux", "az4"), lambda: up_along_z((2,))),
        "vp": (("vz0", "vz1", "vz2", "vz3"), lambda: act_along_x(1 - zlo, "vp")),
        "vq": (("vz4",), act_late),
        "fin": (("both4",), finish),
    }
    for k in (2, 3, 4):
        events[f"az{k}"] = ((f"az{k - 1}",), functools.partial(a_along_z, k))
    for h in (0, 1):
        events[f"bz1{h}"] = (("by", "bf") if h else ("by",), functools.partial(b_along_z, 1, h))
        for k in (2, 3):
            events[f"bz{k}{h}"] = ((f"bz{k - 1}{h}",), functools.partial(b_along_z, k, h))
    for dz in range(8):
        k = min(dz, 8 - dz)
        lower = {0: ("by", "bf"), 4: ("bz4",)}.get(k, (f"bz{k}0", f"bz{k}1"))
        upper = {0: ("uz0",), 1: ("uz0", "uz1"), 2: ("uz1",), 3: ("uz1", "uz2"), 4: ("uz2",)}[k]
        if dz:
            events[f"ay{dz}"] = ((f"az{k}",), functools.partial(a_along_y, dz))
        events[f"af{dz}"] = ((f"ay{dz}",), functools.partial(a_far_y, dz))
        events[f"f{dz}"] = (("w", f"af{dz}") + lower, functools.partial(forward, dz))
        events[f"s{dz}"] = ((f"pair{dz}",), functools.partial(scatter, dz))
        events[f"m{dz}"] = ((f"sum{dz}",) + upper, functools.partial(middle, dz))
        events[f"r{dz}"] = ((f"near{dz}",), functools.partial(relay, dz))
        events[f"p{dz}"] = ((f"grad{dz}",), functools.partial(pass_on, dz))
        events[f"b{dz}"] = ((f"both{dz}",), functools.partial(backward, dz))
    events["f4"] = (events["f4"][0], forward_last)
    for delta in range(4):
        events[f"vz{delta}"] = ((), functools.partial(act_along_z, delta))
    events["vz2"] = ((), functools.partial(act_half_along_z, 1 - zlo, "va"))
    events["vz4"] = ((), functools.partial(act_half_along_z, zlo, "vb"))
    received["vz0"] = act_stay.wait
    received["vz2"] = functools.partial(act_half_from_z, 1 - zlo, "va")
    received["vz4"] = functools.partial(act_half_from_z, zlo, "vb")

    had = set()

    def need(name):
        if name not in had:
            had.add(name)
            received[name]()

    for name in ORDER:
        needs, do = events[name]
        for other in needs:
            need(other)
        do()
    act_done()
    for tile in range(FEAT // TILE):
        for c in stores(tile):
            c.wait()
    for c in last_tok + last_grad:
        c.wait()
    for c in sent.values():
        c.wait_send()
    assert len(numbers) <= NSEM, len(numbers)


def update(act_in, tok_ref, grad_ref, sum_ref, w_ref, m_ref, act_out, nw_ref, nm_ref, act_sem):
    step = pl.program_id(0)
    act = pltpu.make_async_copy(act_in, act_out, act_sem)

    @pl.when(step == 0)
    def _():
        act.start()

    grad_sum = sum_ref[...] + lax.dot_general(
        tok_ref[...], grad_ref[...], (((0,), (0,)), ((), ())), preferred_element_type=jnp.float32
    )
    moment_f = m_ref[...].astype(jnp.float32)
    weight_f = w_ref[...].astype(jnp.float32)
    blended = beta_one * moment_f + ((1.0 - beta_one) * fan_scale) * grad_sum
    sign = blended * lax.rsqrt(blended * blended + smooth_tau * smooth_tau)
    nw_ref[...] = ((1.0 - lion_rate * decay_rate) * weight_f - lion_rate * sign).astype(jnp.bfloat16)
    nm_ref[...] = (beta_two * moment_f + ((1.0 - beta_two) * fan_scale) * grad_sum).astype(jnp.bfloat16)

    @pl.when(step == pl.num_programs(0) - 1)
    def _():
        act.wait()


def shards(tokens, weight, moment, upstream):
    bf16, f32 = jnp.bfloat16, jnp.float32
    any_space = pl.BlockSpec(memory_space=pl.ANY)
    act_shape = jax.ShapeDtypeStruct((2, 4, TOK, HALF), bf16)
    block_shape = jax.ShapeDtypeStruct((FEAT, HID), bf16)
    act, grad_sum, last_tok, last_grad = pl.pallas_call(
        kernel,
        out_shape=(
            act_shape,
            jax.ShapeDtypeStruct((FEAT, HID), f32),
            jax.ShapeDtypeStruct((PIECE, FEAT), bf16),
            jax.ShapeDtypeStruct((PIECE, HID), bf16),
        ),
        in_specs=[any_space] * 3,
        out_specs=(any_space,) * 4,
        scratch_shapes=[
            pltpu.VMEM((8, PIECE, KA), bf16),
            pltpu.VMEM((8, PIECE, KB), bf16),
            pltpu.VMEM((FEAT, HID), bf16),
            pltpu.VMEM((FEAT, HID), f32),
            pltpu.VMEM((8, PIECE, HALF), f32),
            pltpu.VMEM((8, PIECE, HALF), bf16),
            pltpu.VMEM((8, PIECE, HALF), bf16),
            pltpu.VMEM((8, PIECE, HALF), bf16),
            pltpu.VMEM((8, 3, TOK, HALF), bf16),
            pltpu.VMEM((8, 2, PIECE, HALF), bf16),
            pltpu.VMEM((4, 2, TOK, HALF), bf16),
            pltpu.VMEM((4, 2, TOK, HALF), bf16),
            pltpu.VMEM((4, 2, TOK, HALF), bf16),
            pltpu.VMEM((4, 2, TOK, HALF), bf16),
            pltpu.SemaphoreType.DMA((NSEM,)),
            pltpu.SemaphoreType.DMA((NSEM,)),
            pltpu.SemaphoreType.DMA((6,)),
            pltpu.SemaphoreType.DMA((FEAT // 256, 2)),
            pltpu.SemaphoreType.DMA((2,)),
            pltpu.SemaphoreType.DMA((4,)),
        ],
        compiler_params=pltpu.CompilerParams(
            collective_id=0, has_side_effects=True, vmem_limit_bytes=44 * 1024 * 1024
        ),
        cost_estimate=pl.CostEstimate(
            flops=4 * 2048 * FEAT * HID, bytes_accessed=12 * 1024 * 1024, transcendentals=2 * FEAT * HID
        ),
    )(tokens, weight, upstream.reshape(2, 4, TOK, HALF))
    tile = pl.BlockSpec((UPDATE, HID), lambda t: (t, 0))
    act, new_weight, new_moment = pl.pallas_call(
        update,
        out_shape=(act_shape, block_shape, block_shape),
        grid=(FEAT // UPDATE,),
        in_specs=[
            any_space,
            pl.BlockSpec((PIECE, UPDATE), lambda t: (0, t)),
            pl.BlockSpec((PIECE, HID), lambda t: (0, 0)),
            tile,
            tile,
            tile,
        ],
        out_specs=(any_space, tile, tile),
        scratch_shapes=[pltpu.SemaphoreType.DMA],
        compiler_params=pltpu.CompilerParams(vmem_limit_bytes=16 * 1024 * 1024),
        cost_estimate=pl.CostEstimate(
            flops=2 * PIECE * FEAT * HID, bytes_accessed=16 * FEAT * HID, transcendentals=FEAT * HID
        ),
    )(act, last_tok, last_grad, grad_sum, weight, moment)
    return (act.reshape(upstream.shape), new_weight, new_moment)


def solution(mesh):
    placed = (
        P(("row", "col"), "depth"),
        P("depth", ("row", "col")),
        P("depth", ("row", "col")),
        P(None, "col", ("row", "depth")),
    )
    return jax.shard_map(
        shards,
        mesh=mesh,
        in_specs=placed,
        out_specs=(
            P(None, "col", ("row", "depth")),
            P("depth", ("row", "col")),
            P("depth", ("row", "col")),
        ),
        check_vma=False,
    )
```

```python
import functools

import jax
import jax.numpy as jnp
from jax import lax
from jax.experimental import pallas as pl
from jax.experimental.pallas import tpu as pltpu
from jax.sharding import PartitionSpec as P

D = 12288
TOK = 64
KA = 1024
KB = 512
FEAT = 1536
HID = 768
HALF = 384
PIECE = 256
NSEM = 176
UPDATE = 256

gelu_coef = 0.7978845608028654
cubic_coef = 0.044715
lion_rate = 0.5
decay_rate = 0.1
beta_one = 0.9
beta_two = 0.99
smooth_tau = 0.1
fan_scale = D ** (-0.5)

MESH = pl.DeviceIdType.MESH

ORDER = (
    "start", "bfar", "bz10", "ay7", "az2", "ay1", "u0", "af0", "bz11", "bz20", "af7", "az3", "uz1", "ay2", "af1",
    "ay6", "bz21", "f0", "f7", "s0", "bz30", "s7", "af2", "ay3", "az4", "ay5", "f1", "m0", "s1", "af6", "m7", "r0",
    "bz31", "f2", "af3", "m1", "r7", "vz0", "p0", "s2", "af5", "b0", "f6", "ay4", "uz2", "p7", "r1", "bz4", "s6",
    "f3", "f5", "m2", "b7", "af4", "s3", "p1", "s5", "m6", "b1", "r2", "f4", "m3", "vz1", "s4", "m5", "vz3", "vz2",
    "r6", "p2", "r3", "b2", "m4", "vz4", "r5", "p6", "p3", "vp", "b6", "r4", "b3", "vq", "p5", "p4", "b5", "fin",
)


def gelu_pair(preact):
    tangent = jnp.tanh(gelu_coef * (preact + cubic_coef * preact * preact * preact))
    gelu_value = 0.5 * preact * (1.0 + tangent)
    gelu_slope = 0.5 * (1.0 + tangent) + 0.5 * preact * (1.0 - tangent * tangent) * gelu_coef * (
        1.0 + 3.0 * cubic_coef * preact * preact
    )
    return (gelu_value, gelu_slope)


def kernel(
    tok_hbm, w_hbm, up_hbm,
    act_hbm, grad_hbm, last_tok_hbm, last_grad_hbm,
    xa, xb, wv, acc, own, give, got, part, share, grads, up1, up2, val2, val1,
    send_sem, recv_sem, load_sem, store_sem, act_sem, last_sem,
):
    row, col, depth = lax.axis_index("row"), lax.axis_index("col"), lax.axis_index("depth")
    y, zlo = lax.rem(row, 4), row // 4
    z = col * 2 + zlo
    x, core = depth // 2, lax.rem(depth, 2)

    def at(y_, z_, x_, core_):
        return (lax.rem(z_, 2) * 4 + y_, z_ // 2, x_ * 2 + core_)

    def y_to(k):
        return at(lax.rem(y + k, 4), z, x, core)

    def z_to(k):
        return at(y, lax.rem(z + k, 8), x, core)

    def x_to(k):
        return at(y, z, lax.rem(x + k, 4), core)

    def col_to(k):
        return (row, lax.rem(col + k, 4), depth)

    partner = at(y, z, x, 1 - core)
    numbers = {}
    sent = {}

    def copy(name, src, dst, device):
        n = numbers.setdefault(name, len(numbers))
        return pltpu.make_async_remote_copy(
            src_ref=src, dst_ref=dst, send_sem=send_sem.at[n], recv_sem=recv_sem.at[n],
            device_id=device, device_id_type=MESH,
        )

    def send(name, src, dst, device):
        c = copy(name, src, dst, device)
        c.start()
        sent[name] = c

    def arrive(name, dst):
        copy(name, dst, dst, partner).wait_recv()

    mine = pl.ds(pl.multiple_of(core * HALF, 128), HALF)
    theirs = pl.ds(pl.multiple_of((1 - core) * HALF, 128), HALF)
    halves = ((mine, pl.ds(0, HALF)), (theirs, pl.ds(HALF, HALF)))
    loads = [
        pltpu.make_async_copy(tok_hbm.at[:, pl.ds(0, KA)], xa.at[0, pl.ds(0, TOK)], load_sem.at[0]),
        pltpu.make_async_copy(tok_hbm.at[:, pl.ds(KA, KB)], xb.at[0, pl.ds(0, TOK)], load_sem.at[1]),
    ]
    for i, (there, here) in enumerate(halves):
        loads.append(pltpu.make_async_copy(w_hbm.at[:, there], wv.at[:, here], load_sem.at[2 + i]))

    def home_row(x_of, x_home):
        return lax.rem(y + x_of + col + 4 - x_home, 4)

    loads.append(pltpu.make_async_copy(up_hbm.at[:, home_row(x, x)], up1.at[x], load_sem.at[4]))
    for c in loads:
        c.start()

    barrier = pltpu.get_barrier_semaphore()
    others = (
        [y_to(1), y_to(3), z_to(1), z_to(7), partner]
        + [x_to(k) for k in (1, 2, 3)]
    )
    for other in others:
        pl.semaphore_signal(barrier, inc=1, device_id=other, device_id_type=MESH)
    pl.semaphore_wait(barrier, len(others))

    LOW, HIGH = pl.ds(0, 32), pl.ds(32, 32)

    def rows(dy, lo=0, n=TOK):
        return pl.ds(dy * TOK + lo, n)

    def a_along_z(k):
        down, up = (k - 1) % 8, (1 - k) % 8
        if k < 4:
            send(("az-", k), xa.at[down, rows(0)], xa.at[k, rows(0)], z_to(7))
            send(("az+", k), xa.at[up, rows(0)], xa.at[8 - k, rows(0)], z_to(1))
        else:
            send(("az-", 4), xa.at[3, LOW], xa.at[4, LOW], z_to(7))
            send(("az+", 4), xa.at[5, HIGH], xa.at[4, HIGH], z_to(1))

    def a_from_z(k):
        if k < 4:
            arrive(("az-", k), xa.at[k, rows(0)])
            arrive(("az+", k), xa.at[8 - k, rows(0)])
        else:
            arrive(("az-", 4), xa.at[4, LOW])
            arrive(("az+", 4), xa.at[4, HIGH])

    def a_along_y(dz):
        send(("ay-", dz), xa.at[dz, rows(0)], xa.at[dz, rows(1)], y_to(3))
        send(("ay+", dz), xa.at[dz, rows(0)], xa.at[dz, rows(3)], y_to(1))

    def a_from_y(dz):
        arrive(("ay-", dz), xa.at[dz, rows(1)])
        arrive(("ay+", dz), xa.at[dz, rows(3)])

    def a_far_y(dz):
        send(("af-", dz), xa.at[dz, rows(1, 0, 32)], xa.at[dz, rows(2, 0, 32)], y_to(3))
        send(("af+", dz), xa.at[dz, rows(3, 32, 32)], xa.at[dz, rows(2, 32, 32)], y_to(1))

    def a_from_far(dz):
        arrive(("af-", dz), xa.at[dz, rows(2, 0, 32)])
        arrive(("af+", dz), xa.at[dz, rows(2, 32, 32)])

    def b_along_y():
        send("by-", xb.at[0, rows(0)], xb.at[0, rows(1)], y_to(3))
        send("by+", xb.at[0, rows(0)], xb.at[0, rows(3)], y_to(1))

    def b_from_y():
        arrive("by-", xb.at[0, rows(1)])
        arrive("by+", xb.at[0, rows(3)])

    def b_far_y():
        send("bf-", xb.at[0, rows(1, 0, 32)], xb.at[0, rows(2, 0, 32)], y_to(3))
        send("bf+", xb.at[0, rows(3, 32, 32)], xb.at[0, rows(2, 32, 32)], y_to(1))

    def b_from_far():
        arrive("bf-", xb.at[0, rows(2, 0, 32)])
        arrive("bf+", xb.at[0, rows(2, 32, 32)])

    HALVES = (pl.ds(0, 128), pl.ds(128, 128))

    def b_along_z(k, h):
        down, up, part_rows = (k - 1) % 8, (1 - k) % 8, HALVES[h]
        send(("bz-", k, h), xb.at[down, part_rows], xb.at[k, part_rows], z_to(7))
        send(("bz+", k, h), xb.at[up, part_rows], xb.at[8 - k, part_rows], z_to(1))

    def b_from_z(k, h):
        arrive(("bz-", k, h), xb.at[k, HALVES[h]])
        arrive(("bz+", k, h), xb.at[8 - k, HALVES[h]])

    def b_far_z():
        send("bq-", xb.at[3, HALVES[0]], xb.at[4, HALVES[0]], z_to(7))
        send("bq+", xb.at[5, HALVES[1]], xb.at[4, HALVES[1]], z_to(1))

    def b_from_far_z():
        arrive("bq-", xb.at[4, HALVES[0]])
        arrive("bq+", xb.at[4, HALVES[1]])

    def up_along_x():
        for k in (1, 2, 3):
            there = lax.rem(x + k, 4)
            send(("ux", k), up_hbm.at[:, home_row(there, x)], up1.at[x], x_to(k))

    def up_from_x():
        loads[4].wait()
        for k in (1, 2, 3):
            arrive(("ux", k), up1.at[lax.rem(x + 4 - k, 4)])

    stay = pltpu.make_async_copy(up1.at[col], up2.at[0], load_sem.at[5])

    def up_along_z(ks):
        for k in ks:
            send(("uz", k), up1.at[lax.rem(col + k, 4)], up2.at[4 - k], col_to(k))

    def up_from_z(ks):
        for k in ks:
            arrive(("uz", k), up2.at[4 - k])

    def act_along_z(delta):
        if delta == 0:
            act_stay.start()
        else:
            send(("vz", delta), val2.at[delta], val1.at[col], col_to(delta))

    def act_half_along_z(odd, name):
        send((name, 2), val2.at[2, odd], val1.at[col, odd], col_to(2))

    def act_from_z(delta):
        arrive(("vz", delta), val1.at[lax.rem(col + 4 - delta, 4)])

    def act_half_from_z(odd, name):
        arrive((name, 2), val1.at[lax.rem(col + 2, 4), odd])

    def act_along_x(odd, name):
        for k in (1, 2, 3):
            there = lax.rem(x + k, 4)
            send((name, k), val1.at[there, odd], act_hbm.at[odd, home_row(x, there)], x_to(k))

    act_stay = pltpu.make_async_copy(val2.at[0], val1.at[col], act_sem.at[0])
    act_here = pltpu.make_async_copy(val1.at[x], act_hbm.at[:, home_row(x, x)], act_sem.at[1])

    def act_late():
        act_along_x(zlo, "vq")
        act_here.start()

    def act_done():
        act_here.wait()
        for odd, name in ((1 - zlo, "vp"), (zlo, "vq")):
            for k in (1, 2, 3):
                arrive((name, k), act_hbm.at[odd, home_row(lax.rem(x + 4 - k, 4), x)])

    def delta_of(dz):
        return lax.rem((zlo + dz) // 2, 4)

    def chunk_rows(dz, x_of):
        dy = lax.rem(x_of + delta_of(dz), 4)
        return pl.ds(pl.multiple_of(dy * TOK, TOK), TOK)

    def forward(dz):
        for n in range(3):
            columns = pl.ds(n * 256, 256)
            value = jnp.dot(xa[dz], wv[pl.ds(0, KA), columns], preferred_element_type=jnp.float32)
            value = value + jnp.dot(xb[dz], wv[pl.ds(KA, KB), columns], preferred_element_type=jnp.float32)
            if n == 0:
                own[dz, :, pl.ds(0, 256)] = value
            elif n == 1:
                own[dz, :, pl.ds(256, 128)] = value[:, :128]
                give[dz, :, pl.ds(0, 128)] = value[:, 128:].astype(jnp.bfloat16)
            else:
                give[dz, :, pl.ds(128, 256)] = value.astype(jnp.bfloat16)
        send(("pair", dz), give.at[dz], got.at[dz], partner)

    def scatter(dz):
        total = own[dz] + got[dz].astype(jnp.float32)
        own[dz] = total
        part[dz] = total.astype(jnp.bfloat16)
        for k in (1, 2, 3):
            chunk = chunk_rows(dz, lax.rem(x + k, 4))
            send(("sum", dz, k), part.at[dz, chunk], share.at[dz, k - 1], x_to(k))

    def middle(dz):
        chunk = chunk_rows(dz, x)
        summed = own[dz, chunk, :]
        for k in range(3):
            summed = summed + share[dz, k].astype(jnp.float32)
        gelu_value, gelu_slope = gelu_pair(summed * fan_scale)
        delta, odd = delta_of(dz), lax.rem(zlo + dz, 2)
        val2[delta, odd] = gelu_value.astype(jnp.bfloat16)
        grads[dz, 0, chunk, :] = (up2[delta, odd].astype(jnp.float32) * gelu_slope).astype(jnp.bfloat16)
        for k in (1, 3):
            send(("grad", dz, k), grads.at[dz, 0, chunk], grads.at[dz, 0, chunk], x_to(k))

    def half_chunk(dz, x_of, lo):
        dy = lax.rem(x_of + delta_of(dz), 4)
        return pl.ds(pl.multiple_of(dy * TOK + lo, 32), 32)

    def relay(dz):
        low, high = half_chunk(dz, lax.rem(x + 3, 4), 0), half_chunk(dz, lax.rem(x + 1, 4), 32)
        send(("far", dz, 1), grads.at[dz, 0, low], grads.at[dz, 0, low], x_to(1))
        send(("far", dz, 3), grads.at[dz, 0, high], grads.at[dz, 0, high], x_to(3))

    def far_from(dz):
        far = lax.rem(x + 2, 4)
        arrive(("far", dz, 1), grads.at[dz, 0, half_chunk(dz, far, 0)])
        arrive(("far", dz, 3), grads.at[dz, 0, half_chunk(dz, far, 32)])

    def pass_on(dz):
        send(("both", dz), grads.at[dz, 0], grads.at[dz, 1], partner)

    def gradient_tile(dz, tile):
        both = jnp.concatenate([grads[dz, 0], grads[dz, 1]], axis=1)
        if isinstance(tile, tuple):
            source, columns = tile
        return lax.dot_general(
            source[dz, :, columns], both, (((0,), (0,)), ((), ())), preferred_element_type=jnp.float32
        )

    TILE = 256
    begun = []

    def backward(dz):
        first = not begun
        begun.append(dz)
        last = len(begun) == 7

        for source, base, count in ((xa, 0, KA // TILE), (xb, KA, KB // TILE)):
            @pl.loop(0, count)
            def _(t):
                columns = pl.ds(pl.multiple_of(t * TILE, TILE), TILE)
                out = pl.ds(pl.multiple_of(base + t * TILE, TILE), TILE)
                value = gradient_tile(dz, (source, columns))
                acc[out, :] = value if first else acc[out, :] + value
                if last:
                    for c in stores(base // TILE + t):
                        c.start()

    def stores(tile):
        out = pl.ds(pl.multiple_of(tile * TILE, TILE), TILE)
        result = []
        for i, (there, here) in enumerate(halves):
            result.append(pltpu.make_async_copy(acc.at[out, here], grad_hbm.at[out, there], store_sem.at[tile, i]))
        return result

    last_tok = [
        pltpu.make_async_copy(xa.at[4], last_tok_hbm.at[:, pl.ds(0, KA)], last_sem.at[0]),
        pltpu.make_async_copy(xb.at[4], last_tok_hbm.at[:, pl.ds(KA, KB)], last_sem.at[1]),
    ]
    last_grad = [
        pltpu.make_async_copy(grads.at[4, 0], last_grad_hbm.at[:, mine], last_sem.at[2]),
        pltpu.make_async_copy(grads.at[4, 1], last_grad_hbm.at[:, theirs], last_sem.at[3]),
    ]

    def forward_last():
        forward(4)
        for c in last_tok:
            c.start()

    def finish():
        for c in last_grad:
            c.start()

    def sums_from(dz):
        for k in (1, 2, 3):
            arrive(("sum", dz, k), share.at[dz, k - 1])

    def grads_from(dz):
        for k in (1, 3):
            arrive(("grad", dz, k), grads.at[dz, 0, chunk_rows(dz, lax.rem(x + 4 - k, 4))])

    def wait_all(copies):
        for c in copies:
            c.wait()

    received = {
        "tok_a": loads[0].wait, "tok_b": loads[1].wait, "by": b_from_y, "bf": b_from_far, "bz4": b_from_far_z,
        "ux": up_from_x, "uz0": stay.wait, "uz1": lambda: up_from_z((1, 3)), "uz2": lambda: up_from_z((2,)),
        "w": lambda: wait_all(loads[2:4]),
    }
    for k in (1, 2, 3, 4):
        received[f"az{k}"] = functools.partial(a_from_z, k)
        for h in (0, 1):
            received[f"bz{k}{h}"] = functools.partial(b_from_z, k, h)
    for dz in range(8):
        received[f"ay{dz}"] = functools.partial(a_from_y, dz)
        received[f"af{dz}"] = functools.partial(a_from_far, dz)
        received[f"pair{dz}"] = functools.partial(lambda d: arrive(("pair", d), got.at[d]), dz)
        received[f"sum{dz}"] = functools.partial(sums_from, dz)
        received[f"near{dz}"] = functools.partial(grads_from, dz)
        received[f"grad{dz}"] = functools.partial(far_from, dz)
        received[f"both{dz}"] = functools.partial(lambda d: arrive(("both", d), grads.at[d, 1]), dz)
    for delta in (1, 2, 3):
        received[f"vz{delta}"] = functools.partial(act_from_z, delta)

    def begin():
        need("tok_a")
        a_along_z(1)
        need("tok_b")
        b_along_y()
        a_along_y(0)
        up_along_x()

    events = {
        "start": ((), begin),
        "bfar": (("by",), b_far_y),
        "bz4": (("bz30", "bz31"), b_far_z),
        "u0": (("ux",), stay.start),
        "uz1": (("ux", "az2"), lambda: up_along_z((1, 3))),
        "uz2": (("ux", "az4"), lambda: up_along_z((2,))),
        "vp": (("vz0", "vz1", "vz2", "vz3"), lambda: act_along_x(1 - zlo, "vp")),
        "vq": (("vz4",), act_late),
        "fin": (("both4",), finish),
    }
    for k in (2, 3, 4):
        events[f"az{k}"] = ((f"az{k - 1}",), functools.partial(a_along_z, k))
    for h in (0, 1):
        events[f"bz1{h}"] = (("by", "bf") if h else ("by",), functools.partial(b_along_z, 1, h))
        for k in (2, 3):
            events[f"bz{k}{h}"] = ((f"bz{k - 1}{h}",), functools.partial(b_along_z, k, h))
    for dz in range(8):
        k = min(dz, 8 - dz)
        lower = {0: ("by", "bf"), 4: ("bz4",)}.get(k, (f"bz{k}0", f"bz{k}1"))
        upper = {0: ("uz0",), 1: ("uz0", "uz1"), 2: ("uz1",), 3: ("uz1", "uz2"), 4: ("uz2",)}[k]
        if dz:
            events[f"ay{dz}"] = ((f"az{k}",), functools.partial(a_along_y, dz))
        events[f"af{dz}"] = ((f"ay{dz}",), functools.partial(a_far_y, dz))
        events[f"f{dz}"] = (("w", f"af{dz}") + lower, functools.partial(forward, dz))
        events[f"s{dz}"] = ((f"pair{dz}",), functools.partial(scatter, dz))
        events[f"m{dz}"] = ((f"sum{dz}",) + upper, functools.partial(middle, dz))
        events[f"r{dz}"] = ((f"near{dz}",), functools.partial(relay, dz))
        events[f"p{dz}"] = ((f"grad{dz}",), functools.partial(pass_on, dz))
        events[f"b{dz}"] = ((f"both{dz}",), functools.partial(backward, dz))
    events["f4"] = (events["f4"][0], forward_last)
    for delta in range(4):
        events[f"vz{delta}"] = ((), functools.partial(act_along_z, delta))
    events["vz2"] = ((), functools.partial(act_half_along_z, 1 - zlo, "va"))
    events["vz4"] = ((), functools.partial(act_half_along_z, zlo, "vb"))
    received["vz0"] = act_stay.wait
    received["vz2"] = functools.partial(act_half_from_z, 1 - zlo, "va")
    received["vz4"] = functools.partial(act_half_from_z, zlo, "vb")

    had = set()

    def need(name):
        if name not in had:
            had.add(name)
            received[name]()

    for name in ORDER:
        needs, do = events[name]
        for other in needs:
            need(other)
        do()
    act_done()
    for tile in range(FEAT // TILE):
        for c in stores(tile):
            c.wait()
    for c in last_tok + last_grad:
        c.wait()
    for c in sent.values():
        c.wait_send()
    assert len(numbers) <= NSEM, len(numbers)


def update(act_in, tok_ref, grad_ref, sum_ref, w_ref, m_ref, act_out, nw_ref, nm_ref, act_sem):
    step = pl.program_id(0)
    act = pltpu.make_async_copy(act_in, act_out, act_sem)

    @pl.when(step == 0)
    def _():
        act.start()

    grad_sum = sum_ref[...] + lax.dot_general(
        tok_ref[...], grad_ref[...], (((0,), (0,)), ((), ())), preferred_element_type=jnp.float32
    )
    moment_f = m_ref[...].astype(jnp.float32)
    weight_f = w_ref[...].astype(jnp.float32)
    blended = beta_one * moment_f + ((1.0 - beta_one) * fan_scale) * grad_sum
    sign = blended * lax.rsqrt(blended * blended + smooth_tau * smooth_tau)
    nw_ref[...] = ((1.0 - lion_rate * decay_rate) * weight_f - lion_rate * sign).astype(jnp.bfloat16)
    nm_ref[...] = (beta_two * moment_f + ((1.0 - beta_two) * fan_scale) * grad_sum).astype(jnp.bfloat16)

    @pl.when(step == pl.num_programs(0) - 1)
    def _():
        act.wait()


def shards(tokens, weight, moment, upstream):
    bf16, f32 = jnp.bfloat16, jnp.float32
    any_space = pl.BlockSpec(memory_space=pl.ANY)
    act_shape = jax.ShapeDtypeStruct((2, 4, TOK, HALF), bf16)
    block_shape = jax.ShapeDtypeStruct((FEAT, HID), bf16)
    act, grad_sum, last_tok, last_grad = pl.pallas_call(
        kernel,
        out_shape=(
            act_shape,
            jax.ShapeDtypeStruct((FEAT, HID), f32),
            jax.ShapeDtypeStruct((PIECE, FEAT), bf16),
            jax.ShapeDtypeStruct((PIECE, HID), bf16),
        ),
        in_specs=[any_space] * 3,
        out_specs=(any_space,) * 4,
        scratch_shapes=[
            pltpu.VMEM((8, PIECE, KA), bf16),
            pltpu.VMEM((8, PIECE, KB), bf16),
            pltpu.VMEM((FEAT, HID), bf16),
            pltpu.VMEM((FEAT, HID), f32),
            pltpu.VMEM((8, PIECE, HALF), f32),
            pltpu.VMEM((8, PIECE, HALF), bf16),
            pltpu.VMEM((8, PIECE, HALF), bf16),
            pltpu.VMEM((8, PIECE, HALF), bf16),
            pltpu.VMEM((8, 3, TOK, HALF), bf16),
            pltpu.VMEM((8, 2, PIECE, HALF), bf16),
            pltpu.VMEM((4, 2, TOK, HALF), bf16),
            pltpu.VMEM((4, 2, TOK, HALF), bf16),
            pltpu.VMEM((4, 2, TOK, HALF), bf16),
            pltpu.VMEM((4, 2, TOK, HALF), bf16),
            pltpu.SemaphoreType.DMA((NSEM,)),
            pltpu.SemaphoreType.DMA((NSEM,)),
            pltpu.SemaphoreType.DMA((6,)),
            pltpu.SemaphoreType.DMA((FEAT // 256, 2)),
            pltpu.SemaphoreType.DMA((2,)),
            pltpu.SemaphoreType.DMA((4,)),
        ],
        compiler_params=pltpu.CompilerParams(
            collective_id=0, has_side_effects=True, vmem_limit_bytes=44 * 1024 * 1024
        ),
        cost_estimate=pl.CostEstimate(
            flops=4 * 2048 * FEAT * HID, bytes_accessed=12 * 1024 * 1024, transcendentals=2 * FEAT * HID
        ),
    )(tokens, weight, upstream.reshape(2, 4, TOK, HALF))
    tile = pl.BlockSpec((UPDATE, HID), lambda t: (t, 0))
    act, new_weight, new_moment = pl.pallas_call(
        update,
        out_shape=(act_shape, block_shape, block_shape),
        grid=(FEAT // UPDATE,),
        in_specs=[
            any_space,
            pl.BlockSpec((PIECE, UPDATE), lambda t: (0, t)),
            pl.BlockSpec((PIECE, HID), lambda t: (0, 0)),
            tile,
            tile,
            tile,
        ],
        out_specs=(any_space, tile, tile),
        scratch_shapes=[pltpu.SemaphoreType.DMA],
        compiler_params=pltpu.CompilerParams(vmem_limit_bytes=16 * 1024 * 1024),
        cost_estimate=pl.CostEstimate(
            flops=2 * PIECE * FEAT * HID, bytes_accessed=16 * FEAT * HID, transcendentals=FEAT * HID
        ),
    )(act, last_tok, last_grad, grad_sum, weight, moment)
    return (act.reshape(upstream.shape), new_weight, new_moment)


def solution(mesh):
    placed = (
        P(("row", "col"), "depth"),
        P("depth", ("row", "col")),
        P("depth", ("row", "col")),
        P(None, "col", ("row", "depth")),
    )
    return jax.shard_map(
        shards,
        mesh=mesh,
        in_specs=placed,
        out_specs=(
            P(None, "col", ("row", "depth")),
            P("depth", ("row", "col")),
            P("depth", ("row", "col")),
        ),
        check_vma=False,
    )
```
